32 devices in a mesh: section: 4 (over y, x), seq: 8 (over z, core).
Axes of the slice: x: 2, y: 2, z: 4, core: 2. Of those that a mesh axis runs over, the one named last changes fastest.
Arguments:
- span_inputs: bfloat16 [4, 256, 3, 8192], P('section', 'seq'), may hold values from -28 to 28
- out_grad: bfloat16 [4, 256, 8192], P('section', 'seq'), may hold values from -48 to 48
- past_cache: bfloat16 [4, 384, 2, 64, 128], P('section', None, None, 'seq'), may hold values from -5 to 5
- past_accum: float32 [4, 384, 2, 64, 128], P('section', None, None, 'seq'), may hold values from -0.6 to 0.6
- offsets: int32 [4], P('section'), may hold values from 0 to 384, as said below
- lengths: int32 [4], P('section'), may hold values from 128 to 256, as said below
Outputs:
- next_grads: bfloat16 [4, 256, 3, 8192], P('section', 'seq')
- new_accum: float32 [4, 384, 2, 64, 128], P('section', None, None, 'seq')
The draws below stay inside these ranges and needn't reach their ends.
Inputs may be any that keep to these rules, and one draw needn't show every extreme that they name: The first offsets[s] rows of past_cache[s] and past_accum[s] belong to the sequence; one section's offset is 384. Rows of a span from lengths[s] on are padding; one section's length is 256.
All inputs are finite; a program needn't handle non-finite values.
Results may differ from the reference program's by a relative error of at most 0.0068.
Values may be sent and summed in bfloat16 or wider, within the bound.
A program may use at most 128 MiB of HBM per device.

```python
import math
import jax
import jax.numpy as jnp
from jax import lax

HEADS = 64
DH = 128
D = 8192
SPAN = 256
PAST = 384
SECTIONS = 4


def draw_span_inputs(key, part):
    base_draw = jnp.clip(jax.random.normal(key, (SECTIONS, SPAN, 3, D), jnp.float32), -5.0, 5.0)
    return base_draw.astype(jnp.bfloat16)


def draw_offsets(key, part):
    first_key, pick_key = jax.random.split(jax.random.fold_in(key, 41))
    drawn = jax.random.randint(first_key, (SECTIONS,), 0, PAST + 1)
    return drawn.at[jax.random.randint(pick_key, (), 0, SECTIONS)].set(PAST).astype(jnp.int32)


def draw_lengths(key, part):
    first_key, pick_key = jax.random.split(jax.random.fold_in(key, 53))
    drawn = jax.random.randint(first_key, (SECTIONS,), SPAN // 2, SPAN + 1)
    return drawn.at[jax.random.randint(pick_key, (), 0, SECTIONS)].set(SPAN).astype(jnp.int32)


def shard_levels(own_key, extent, cuts, smallest, top_value):
    level = 1.0
    for position, parts in cuts:
        draws = jax.random.uniform(jax.random.fold_in(jax.random.fold_in(own_key, 6), position), (parts,), jnp.float32, smallest / len(cuts), top_value / len(cuts))
        level = level * jnp.repeat(jnp.exp(draws), extent[position] // parts).reshape((-1,) + (1,) * (len(extent) - 1 - position))
    return level


def scatter_about(stream_key, extent, width, limit, cuts=(), kind=jnp.bfloat16):
    values = jax.random.normal(stream_key, extent, jnp.float32) * width
    if len(cuts) > 0:
        values = shard_levels(stream_key, extent, cuts, -0.22, 0.18) * values
    return jnp.clip(values, min=-limit, max=limit).astype(kind)


def setup_inputs(seed: int = 0) -> dict:
    key_list = jax.random.split(jax.random.key(seed), 7)
    return {
        "span_inputs": draw_span_inputs(jax.random.fold_in(key_list[6], 71), 0),
        "out_grad": scatter_about(key_list[1], (SECTIONS, SPAN, D), 8.0, 48.0, ((0, 4), (1, 8))),
        "past_cache": scatter_about(key_list[2], (SECTIONS, PAST, 2, HEADS, DH), 1.0, 5.0, ((0, 4), (3, 8))),
        "past_accum": scatter_about(key_list[3], (SECTIONS, PAST, 2, HEADS, DH), 0.1, 0.6, ((0, 4), (3, 8)), jnp.float32),
        "offsets": draw_offsets(jax.random.fold_in(key_list[6], 71), 0),
        "lengths": draw_lengths(jax.random.fold_in(key_list[6], 71), 0),
    }


def head_grads(query_h, keys_h, values_h, dout_h, visible):
    scale_factor = 1.0 / math.sqrt(DH)
    raw_scores = jnp.dot(query_h, keys_h.T, preferred_element_type=jnp.float32) * scale_factor
    masked = jnp.where(visible, raw_scores, -jnp.inf)
    row_max = lax.optimization_barrier(jnp.max(masked, axis=-1, keepdims=True))
    exp_terms = jnp.exp(masked - row_max)
    attention = exp_terms / lax.optimization_barrier(jnp.sum(exp_terms, axis=-1, keepdims=True))
    attention_low = attention.astype(jnp.bfloat16)
    dprobs = jnp.dot(dout_h, values_h.T, preferred_element_type=jnp.float32)
    row_delta = lax.optimization_barrier(jnp.sum(attention * dprobs, axis=-1, keepdims=True))
    dscores = (attention * (dprobs - row_delta)).astype(jnp.bfloat16)
    grad_query = (jnp.dot(dscores, keys_h, preferred_element_type=jnp.float32) * scale_factor).astype(jnp.bfloat16)
    grad_keys = jnp.dot(dscores.T, query_h, preferred_element_type=jnp.float32) * scale_factor
    grad_values = jnp.dot(attention_low.T, dout_h, preferred_element_type=jnp.float32)
    return (grad_query, grad_keys, grad_values)

def section_grads(inputs_now, dout_now, cache_now, accum_now, offset, length):
    local_rows = inputs_now.reshape(SPAN, 3, HEADS, DH)
    positions = jnp.arange(SPAN, dtype=jnp.int32)
    dout_heads = jnp.where((positions < length)[:, None, None], dout_now.reshape(SPAN, HEADS, DH), jnp.zeros((), jnp.bfloat16))
    all_keys = jnp.concatenate([cache_now[:, 0], local_rows[:, 1]], axis=0)
    all_values = jnp.concatenate([cache_now[:, 1], local_rows[:, 2]], axis=0)
    key_index = jnp.arange(PAST + SPAN, dtype=jnp.int32)
    in_span = key_index - PAST
    visible = jnp.where(key_index[None, :] < PAST, key_index[None, :] < offset, (in_span[None, :] <= positions[:, None]) & (in_span[None, :] < length))

    def per_head(items):
        return head_grads(items[0], items[1], items[2], items[3], visible)
    grad_query, grad_keys, grad_values = lax.map(per_head, (jnp.transpose(local_rows[:, 0], (1, 0, 2)), jnp.transpose(all_keys, (1, 0, 2)), jnp.transpose(all_values, (1, 0, 2)), jnp.transpose(dout_heads, (1, 0, 2))))
    span_grads = jnp.stack([grad_query, grad_keys[:, PAST:].astype(jnp.bfloat16), grad_values[:, PAST:].astype(jnp.bfloat16)], axis=0)
    span_grads = jnp.transpose(span_grads, (2, 0, 1, 3)).reshape(SPAN, 3, D)
    added = jnp.transpose(jnp.stack([grad_keys[:, :PAST], grad_values[:, :PAST]], axis=0), (2, 0, 1, 3))
    return (span_grads, accum_now + added)

def reference(span_inputs, out_grad, past_cache, past_accum, offsets, lengths):
    grads_list = []
    accum_list = []
    for section_idx in range(SECTIONS):
        span_grads, accum_new = section_grads(span_inputs[section_idx], out_grad[section_idx], past_cache[section_idx], past_accum[section_idx], offsets[section_idx], lengths[section_idx])
        grads_list.append(span_grads)
        accum_list.append(accum_new)
    next_grads = jnp.roll(jnp.stack(grads_list, axis=0), -1, axis=0)
    return (next_grads, jnp.stack(accum_list, axis=0))
```

```python
import functools
import math

import jax
import jax.numpy as jnp
from jax import lax
from jax.experimental import pallas as pl
from jax.experimental.pallas import tpu as pltpu
from jax.sharding import PartitionSpec as P

DH = 128
MESH = pl.DeviceIdType.MESH
QUERY, KEY, VALUE, DOUT = range(4)


def attention_grads(scale, past, keys, values, query, dout, offset, length, start):
    key_count, rows = keys.shape[0], query.shape[0]
    key_index = lax.broadcasted_iota(jnp.int32, (key_count, rows), 0)
    query_pos = start + lax.broadcasted_iota(jnp.int32, (key_count, rows), 1)
    in_span = key_index - past
    limit = jnp.where(in_span < 0, offset - past, jnp.minimum(query_pos + 1, length))
    over_last = (((1,), (1,)), ((), ()))
    scores = lax.dot_general(keys, query, over_last, preferred_element_type=jnp.float32) * scale
    masked = jnp.where(in_span < limit, scores, -jnp.inf)
    exp_terms = jnp.exp(masked - jnp.max(masked, axis=0, keepdims=True))
    attention = exp_terms * (1.0 / jnp.sum(exp_terms, axis=0, keepdims=True))
    row_pos = start + lax.broadcasted_iota(jnp.int32, (rows, DH), 0)
    dout = jnp.where(row_pos < length, dout, jnp.zeros_like(dout))
    dprobs = lax.dot_general(values, dout, over_last, preferred_element_type=jnp.float32)
    delta = jnp.sum(attention * dprobs, axis=0, keepdims=True)
    dscores = (attention * (dprobs - delta)).astype(jnp.bfloat16)
    grad_values = jnp.dot(
        attention.astype(jnp.bfloat16), dout, preferred_element_type=jnp.float32
    )
    grad_keys = jnp.dot(dscores, query, preferred_element_type=jnp.float32) * scale
    grad_query = (
        lax.dot_general(
            dscores, keys, (((0,), (0,)), ((), ())), preferred_element_type=jnp.float32
        )
        * scale
    )
    return grad_query, grad_keys, grad_values


def kernel(
    dims,
    offset_ref,
    length_ref,
    span_ref,
    dout_ref,
    cache_ref,
    accum_ref,
    grads_ref,
    new_accum_ref,
    held,
    staged,
    cache_low,
    cache_wide,
    accum,
    total_keys,
    total_values,
    send_in,
    recv_in,
    send_out,
    recv_out,
    own_sem,
    io_sem,
):
    sections, n, heads, tok, past, span, chunks, block = dims
    per_chunk = heads // chunks
    scale = 1.0 / math.sqrt(DH)
    me = lax.axis_index("seq")
    section = lax.axis_index("section")
    before = lax.rem(section + sections - 1, sections)
    after = lax.rem(section + 1, sections)

    load_cache = pltpu.make_async_copy(cache_ref, cache_low, io_sem.at[0])
    load_accum = pltpu.make_async_copy(accum_ref, accum, io_sem.at[1])
    load_cache.start()
    load_accum.start()

    def peer_at(k):
        half = n // 2
        mine = me // half
        far = (1 - mine) * half + lax.rem(me + k, half)
        near = mine * half + lax.rem(me + k - half + 1, half)
        return jnp.where(k < half, far, near)

    barrier = pltpu.get_barrier_semaphore()

    def greet_peer(k, carry):
        pl.semaphore_signal(barrier, inc=1, device_id=(section, peer_at(k)), device_id_type=MESH)
        return carry

    def greet_sections(k, carry):
        pl.semaphore_signal(barrier, inc=1, device_id=(before, k), device_id_type=MESH)
        pl.semaphore_signal(barrier, inc=1, device_id=(after, k), device_id_type=MESH)
        return carry

    lax.fori_loop(0, n - 1, greet_peer, 0)
    lax.fori_loop(0, n, greet_sections, 0)
    pl.semaphore_wait(barrier, 3 * n - 1)

    def columns(owner, c):
        return pl.ds(pl.multiple_of((owner * heads + c * per_chunk) * DH, DH), per_chunk * DH)

    def span_rows(owner):
        return pl.ds(pl.multiple_of(past + owner * tok, 16), tok)

    def inputs(c, owner, rows):
        cols = columns(owner, c)
        return (
            (span_ref.at[:, :, cols], held.at[c, pl.ds(0, 3), span_rows(rows), :]),
            (dout_ref.at[:, cols], held.at[c, DOUT, span_rows(rows), :]),
        )

    def send_tokens(c, peer):
        return [
            pltpu.make_async_remote_copy(
                src_ref=source,
                dst_ref=target,
                send_sem=send_in.at[c, which, peer],
                recv_sem=recv_in.at[c, which, me],
                device_id=(section, peer),
                device_id_type=MESH,
            )
            for which, (source, target) in enumerate(inputs(c, peer, me))
        ]

    def receive_tokens(c, peer):
        return [
            pltpu.make_async_remote_copy(
                src_ref=source,
                dst_ref=target,
                send_sem=send_in.at[c, which, me],
                recv_sem=recv_in.at[c, which, peer],
                device_id=(section, peer),
                device_id_type=MESH,
            )
            for which, (source, target) in enumerate(inputs(c, me, peer))
        ]

    def own_tokens(c):
        return [
            pltpu.make_async_copy(source, target, own_sem.at[c, which])
            for which, (source, target) in enumerate(inputs(c, me, me))
        ]

    def send_grads(c, token_owner):
        rows = pl.ds(pl.multiple_of(token_owner * tok, 16), tok)
        return pltpu.make_async_remote_copy(
            src_ref=staged.at[c, :, rows, :],
            dst_ref=grads_ref.at[:, :, columns(me, c)],
            send_sem=send_out.at[c, token_owner],
            recv_sem=recv_out.at[c, me],
            device_id=(before, token_owner),
            device_id_type=MESH,
        )

    def receive_grads(c, head_owner):
        return pltpu.make_async_remote_copy(
            src_ref=staged.at[c, :, pl.ds(0, tok), :],
            dst_ref=grads_ref.at[:, :, columns(head_owner, c)],
            send_sem=send_out.at[c, head_owner],
            recv_sem=recv_out.at[c, head_owner],
            device_id=(after, head_owner),
            device_id_type=MESH,
        )

    def start_chunk(c, carry):
        def start_peer(k, carry):
            for copy in send_tokens(c, peer_at(k)):
                copy.start()
            return carry

        lax.fori_loop(0, n - 1, start_peer, 0)
        for copy in own_tokens(c):
            copy.start()
        return carry

    lax.fori_loop(0, chunks, start_chunk, 0)

    load_cache.wait()
    cache_wide[...] = cache_low[...].astype(jnp.float32)
    for h in range(heads):
        for which in (KEY, VALUE):
            rows = pl.ds((which - KEY) * heads + h, past, stride=2 * heads)
            lanes = pl.ds(h % per_chunk * DH, DH)
            held[h // per_chunk, which, pl.ds(0, past), lanes] = cache_wide[rows, :].astype(jnp.bfloat16)
    load_accum.wait()

    offset = offset_ref[0]
    length = length_ref[0]
    blocks = span // block

    def one_head(c, i):
        h = c * per_chunk + i
        lanes = pl.ds(pl.multiple_of(i * DH, DH), DH)
        keys = held[c, KEY, :, lanes]
        values = held[c, VALUE, :, lanes]

        def one_block(start):
            grad_query, grad_keys, grad_values = attention_grads(
                scale,
                past,
                keys,
                values,
                held[c, QUERY, pl.ds(past + start, block), lanes],
                held[c, DOUT, pl.ds(past + start, block), lanes],
                offset,
                length,
                start,
            )
            staged[c, 0, pl.ds(start, block), lanes] = grad_query.astype(jnp.bfloat16)
            return grad_keys, grad_values

        if blocks == 1:
            grad_keys, grad_values = one_block(0)
        else:
            total_keys[...] = jnp.zeros_like(total_keys)
            total_values[...] = jnp.zeros_like(total_values)

            def step(b, carry):
                more_keys, more_values = one_block(pl.multiple_of(b * block, block))
                total_keys[...] += more_keys
                total_values[...] += more_values
                return carry

            lax.fori_loop(0, blocks, step, 0)
            grad_keys, grad_values = total_keys[...], total_values[...]
        staged[c, 1, :, lanes] = grad_keys[past:].astype(jnp.bfloat16)
        staged[c, 2, :, lanes] = grad_values[past:].astype(jnp.bfloat16)
        accum[pl.ds(h, past, stride=2 * heads), :] += grad_keys[:past]
        accum[pl.ds(heads + h, past, stride=2 * heads), :] += grad_values[:past]

    def work_chunk(c, carry):
        def wait_peer(k, carry):
            for copy in receive_tokens(c, peer_at(k)):
                copy.wait_recv()
            return carry

        lax.fori_loop(0, n - 1, wait_peer, 0)
        for copy in own_tokens(c):
            copy.wait()

        def work_head(i, carry):
            one_head(c, i)
            return carry

        lax.fori_loop(0, per_chunk, work_head, 0)

        def start_out(k, carry):
            send_grads(c, peer_at(k)).start()
            return carry

        lax.fori_loop(0, n - 1, start_out, 0)
        send_grads(c, me).start()
        return carry

    lax.fori_loop(0, chunks, work_chunk, 0)

    store_accum = pltpu.make_async_copy(accum, new_accum_ref, io_sem.at[1])
    store_accum.start()

    def finish_chunk(c, carry):
        def sent(k, carry):
            for copy in send_tokens(c, peer_at(k)):
                copy.wait_send()
            return carry

        def exchanged(t, carry):
            send_grads(c, t).wait_send()
            receive_grads(c, t).wait_recv()
            return carry

        lax.fori_loop(0, n - 1, sent, 0)
        lax.fori_loop(0, n, exchanged, 0)
        return carry

    lax.fori_loop(0, chunks, finish_chunk, 0)
    store_accum.wait()


def per_device(sections, n, span_inputs, out_grad, past_cache, past_accum, offsets, lengths):
    _, tok, _, width = span_inputs.shape
    _, past, _, heads, dh = past_cache.shape
    span = tok * n
    key_count = past + span
    chunks = 4 if heads % 4 == 0 else 1
    block = min(span, 256 if key_count <= 1024 else 128)
    by_kind = span_inputs[0].transpose(1, 0, 2)
    cache_rows = past_cache.reshape(past * 2 * heads, dh)
    accum_rows = past_accum.reshape(past * 2 * heads, dh)
    dims = (sections, n, heads, tok, past, span, chunks, block)
    spread = (key_count, dh) if span > block else (8, dh)
    anywhere = pl.BlockSpec(memory_space=pl.ANY)
    scalar = pl.BlockSpec(memory_space=pltpu.SMEM)
    pairs = heads * span * key_count * dh
    grads, new_rows = pl.pallas_call(
        functools.partial(kernel, dims),
        out_shape=(
            jax.ShapeDtypeStruct((3, tok, width), jnp.bfloat16),
            jax.ShapeDtypeStruct(accum_rows.shape, jnp.float32),
        ),
        in_specs=[scalar, scalar, anywhere, anywhere, anywhere, anywhere],
        out_specs=(anywhere, anywhere),
        scratch_shapes=[
            pltpu.VMEM((chunks, 4, key_count, heads // chunks * dh), jnp.bfloat16),
            pltpu.VMEM((chunks, 3, span, heads // chunks * dh), jnp.bfloat16),
            pltpu.VMEM(cache_rows.shape, jnp.bfloat16),
            pltpu.VMEM(cache_rows.shape, jnp.float32),
            pltpu.VMEM(accum_rows.shape, jnp.float32),
            pltpu.VMEM(spread, jnp.float32),
            pltpu.VMEM(spread, jnp.float32),
            pltpu.SemaphoreType.DMA((chunks, 2, n)),
            pltpu.SemaphoreType.DMA((chunks, 2, n)),
            pltpu.SemaphoreType.DMA((chunks, n)),
            pltpu.SemaphoreType.DMA((chunks, n)),
            pltpu.SemaphoreType.DMA((chunks, 2)),
            pltpu.SemaphoreType.DMA((2,)),
        ],
        compiler_params=pltpu.CompilerParams(
            collective_id=0, has_side_effects=True, vmem_limit_bytes=56 * 1024 * 1024
        ),
        cost_estimate=pl.CostEstimate(
            flops=10 * pairs, bytes_accessed=16 * accum_rows.size, transcendentals=pairs // dh
        ),
    )(offsets, lengths, by_kind, out_grad[0], cache_rows, accum_rows)
    next_grads = grads.transpose(1, 0, 2)[None]
    return next_grads, new_rows.reshape(past_accum.shape)


def solution(mesh):
    in_specs = (
        P("section", "seq", None, None),
        P("section", "seq", None),
        P("section", None, None, "seq", None),
        P("section", None, None, "seq", None),
        P("section"),
        P("section"),
    )
    out_specs = (P("section", "seq", None, None), P("section", None, None, "seq", None))
    return jax.shard_map(
        functools.partial(per_device, mesh.shape["section"], mesh.shape["seq"]),
        mesh=mesh,
        in_specs=in_specs,
        out_specs=out_specs,
        check_vma=False,
    )
```

```python
import functools
import math

import jax
import jax.numpy as jnp
from jax import lax
from jax.experimental import pallas as pl
from jax.experimental.pallas import tpu as pltpu
from jax.sharding import PartitionSpec as P

DH = 128
MESH = pl.DeviceIdType.MESH
QUERY, KEY, VALUE, DOUT = range(4)


def attention_grads(scale, past, keys, values, query, dout, offset, length, start):
    key_count, rows = keys.shape[0], query.shape[0]
    key_index = lax.broadcasted_iota(jnp.int32, (key_count, rows), 0)
    query_pos = start + lax.broadcasted_iota(jnp.int32, (key_count, rows), 1)
    in_span = key_index - past
    limit = jnp.where(in_span < 0, offset - past, jnp.minimum(query_pos + 1, length))
    over_last = (((1,), (1,)), ((), ()))
    scores = lax.dot_general(keys, query, over_last, preferred_element_type=jnp.float32) * scale
    masked = jnp.where(in_span < limit, scores, -jnp.inf)
    exp_terms = jnp.exp(masked - jnp.max(masked, axis=0, keepdims=True))
    attention = exp_terms * (1.0 / jnp.sum(exp_terms, axis=0, keepdims=True))
    row_pos = start + lax.broadcasted_iota(jnp.int32, (rows, DH), 0)
    dout = jnp.where(row_pos < length, dout, jnp.zeros_like(dout))
    dprobs = lax.dot_general(values, dout, over_last, preferred_element_type=jnp.float32)
    delta = jnp.sum(attention * dprobs, axis=0, keepdims=True)
    dscores = (attention * (dprobs - delta)).astype(jnp.bfloat16)
    grad_values = jnp.dot(
        attention.astype(jnp.bfloat16), dout, preferred_element_type=jnp.float32
    )
    grad_keys = jnp.dot(dscores, query, preferred_element_type=jnp.float32) * scale
    grad_query = (
        lax.dot_general(
            dscores, keys, (((0,), (0,)), ((), ())), preferred_element_type=jnp.float32
        )
        * scale
    )
    return grad_query, grad_keys, grad_values


def kernel(
    dims,
    offset_ref,
    length_ref,
    span_ref,
    dout_ref,
    cache_ref,
    accum_ref,
    grads_ref,
    new_accum_ref,
    held,
    staged,
    cache_low,
    cache_wide,
    accum,
    total_keys,
    total_values,
    send_in,
    recv_in,
    send_out,
    recv_out,
    own_sem,
    io_sem,
    small,
):
    sections, n, heads, tok, past, span, chunks, block = dims
    per_chunk = heads // chunks
    scale = 1.0 / math.sqrt(DH)
    me = lax.axis_index("seq")
    section = lax.axis_index("section")
    before = lax.rem(section + sections - 1, sections)
    after = lax.rem(section + 1, sections)

    load_cache = pltpu.make_async_copy(cache_ref, cache_low, io_sem.at[0])
    load_accum = pltpu.make_async_copy(accum_ref, accum, io_sem.at[1])
    load_offset = pltpu.make_async_copy(offset_ref, small.at[0], io_sem.at[2])
    load_length = pltpu.make_async_copy(length_ref, small.at[1], io_sem.at[3])
    load_cache.start()
    load_accum.start()
    load_offset.start()
    load_length.start()

    def peer_at(k):
        half = n // 2
        mine = me // half
        far = (1 - mine) * half + lax.rem(me + k, half)
        near = mine * half + lax.rem(me + k - half + 1, half)
        return jnp.where(k < half, far, near)

    barrier = pltpu.get_barrier_semaphore()

    def greet_peer(k, carry):
        pl.semaphore_signal(barrier, inc=1, device_id=(section, peer_at(k)), device_id_type=MESH)
        return carry

    def greet_sections(k, carry):
        pl.semaphore_signal(barrier, inc=1, device_id=(before, k), device_id_type=MESH)
        pl.semaphore_signal(barrier, inc=1, device_id=(after, k), device_id_type=MESH)
        return carry

    lax.fori_loop(0, n - 1, greet_peer, 0)
    lax.fori_loop(0, n, greet_sections, 0)
    pl.semaphore_wait(barrier, 3 * n - 1)

    def columns(owner, c):
        return pl.ds(pl.multiple_of((owner * heads + c * per_chunk) * DH, DH), per_chunk * DH)

    def span_rows(owner):
        return pl.ds(pl.multiple_of(past + owner * tok, 16), tok)

    def inputs(c, owner, rows):
        cols = columns(owner, c)
        return (
            (span_ref.at[:, :, cols], held.at[c, pl.ds(0, 3), span_rows(rows), :]),
            (dout_ref.at[:, cols], held.at[c, DOUT, span_rows(rows), :]),
        )

    def send_tokens(c, peer):
        return [
            pltpu.make_async_remote_copy(
                src_ref=source,
                dst_ref=target,
                send_sem=send_in.at[c, which, peer],
                recv_sem=recv_in.at[c, which, me],
                device_id=(section, peer),
                device_id_type=MESH,
            )
            for which, (source, target) in enumerate(inputs(c, peer, me))
        ]

    def receive_tokens(c, peer):
        return [
            pltpu.make_async_remote_copy(
                src_ref=source,
                dst_ref=target,
                send_sem=send_in.at[c, which, me],
                recv_sem=recv_in.at[c, which, peer],
                device_id=(section, peer),
                device_id_type=MESH,
            )
            for which, (source, target) in enumerate(inputs(c, me, peer))
        ]

    def own_tokens(c):
        return [
            pltpu.make_async_copy(source, target, own_sem.at[c, which])
            for which, (source, target) in enumerate(inputs(c, me, me))
        ]

    def send_grads(c, token_owner):
        rows = pl.ds(pl.multiple_of(token_owner * tok, 16), tok)
        return pltpu.make_async_remote_copy(
            src_ref=staged.at[c, :, rows, :],
            dst_ref=grads_ref.at[:, :, columns(me, c)],
            send_sem=send_out.at[c, token_owner],
            recv_sem=recv_out.at[c, me],
            device_id=(before, token_owner),
            device_id_type=MESH,
        )

    def receive_grads(c, head_owner):
        return pltpu.make_async_remote_copy(
            src_ref=staged.at[c, :, pl.ds(0, tok), :],
            dst_ref=grads_ref.at[:, :, columns(head_owner, c)],
            send_sem=send_out.at[c, head_owner],
            recv_sem=recv_out.at[c, head_owner],
            device_id=(after, head_owner),
            device_id_type=MESH,
        )

    def start_chunk(c, carry):
        def start_peer(k, carry):
            for copy in send_tokens(c, peer_at(k)):
                copy.start()
            return carry

        lax.fori_loop(0, n - 1, start_peer, 0)
        for copy in own_tokens(c):
            copy.start()
        return carry

    lead = min(2, chunks)
    lax.fori_loop(0, lead, start_chunk, 0)

    load_cache.wait()
    cache_wide[...] = cache_low[...].astype(jnp.float32)
    for h in range(heads):
        for which in (KEY, VALUE):
            rows = pl.ds((which - KEY) * heads + h, past, stride=2 * heads)
            lanes = pl.ds(h % per_chunk * DH, DH)
            held[h // per_chunk, which, pl.ds(0, past), lanes] = cache_wide[rows, :].astype(jnp.bfloat16)
    load_accum.wait()

    load_offset.wait()
    load_length.wait()
    offset = small[0, 0]
    length = small[1, 0]
    blocks = span // block

    def one_head(c, i):
        h = c * per_chunk + i
        lanes = pl.ds(pl.multiple_of(i * DH, DH), DH)
        keys = held[c, KEY, :, lanes]
        values = held[c, VALUE, :, lanes]

        def one_block(start):
            grad_query, grad_keys, grad_values = attention_grads(
                scale,
                past,
                keys,
                values,
                held[c, QUERY, pl.ds(past + start, block), lanes],
                held[c, DOUT, pl.ds(past + start, block), lanes],
                offset,
                length,
                start,
            )
            staged[c, 0, pl.ds(start, block), lanes] = grad_query.astype(jnp.bfloat16)
            return grad_keys, grad_values

        if blocks == 1:
            grad_keys, grad_values = one_block(0)
        else:
            total_keys[...] = jnp.zeros_like(total_keys)
            total_values[...] = jnp.zeros_like(total_values)

            def step(b, carry):
                more_keys, more_values = one_block(pl.multiple_of(b * block, block))
                total_keys[...] += more_keys
                total_values[...] += more_values
                return carry

            lax.fori_loop(0, blocks, step, 0)
            grad_keys, grad_values = total_keys[...], total_values[...]
        staged[c, 1, :, lanes] = grad_keys[past:].astype(jnp.bfloat16)
        staged[c, 2, :, lanes] = grad_values[past:].astype(jnp.bfloat16)
        accum[pl.ds(h, past, stride=2 * heads), :] += grad_keys[:past]
        accum[pl.ds(heads + h, past, stride=2 * heads), :] += grad_values[:past]

    def work_chunk(c, carry):
        def wait_peer(k, carry):
            for copy in receive_tokens(c, peer_at(k)):
                copy.wait_recv()
            return carry

        lax.fori_loop(0, n - 1, wait_peer, 0)
        for copy in own_tokens(c):
            copy.wait()

        def work_head(i, carry):
            one_head(c, i)
            return carry

        lax.fori_loop(0, per_chunk, work_head, 0)

        def start_out(k, carry):
            send_grads(c, peer_at(k)).start()
            return carry

        lax.fori_loop(0, n - 1, start_out, 0)
        send_grads(c, me).start()

        @pl.when(c + lead < chunks)
        def _():
            start_chunk(c + lead, 0)

        return carry

    lax.fori_loop(0, chunks, work_chunk, 0)

    store_accum = pltpu.make_async_copy(accum, new_accum_ref, io_sem.at[1])
    store_accum.start()

    def finish_chunk(c, carry):
        def sent(k, carry):
            for copy in send_tokens(c, peer_at(k)):
                copy.wait_send()
            return carry

        def exchanged(t, carry):
            send_grads(c, t).wait_send()
            receive_grads(c, t).wait_recv()
            return carry

        lax.fori_loop(0, n - 1, sent, 0)
        lax.fori_loop(0, n, exchanged, 0)
        return carry

    lax.fori_loop(0, chunks, finish_chunk, 0)
    store_accum.wait()


def per_device(sections, n, span_inputs, out_grad, past_cache, past_accum, offsets, lengths):
    _, tok, _, width = span_inputs.shape
    _, past, _, heads, dh = past_cache.shape
    span = tok * n
    key_count = past + span
    chunks = 4 if heads % 4 == 0 else 1
    block = min(span, 256 if key_count <= 1024 else 128)
    by_kind = span_inputs[0].transpose(1, 0, 2)
    cache_rows = past_cache.reshape(past * 2 * heads, dh)
    accum_rows = past_accum.reshape(past * 2 * heads, dh)
    dims = (sections, n, heads, tok, past, span, chunks, block)
    spread = (key_count, dh) if span > block else (8, dh)
    anywhere = pl.BlockSpec(memory_space=pl.ANY)
    resident = pl.BlockSpec(memory_space=pltpu.HBM)
    pairs = heads * span * key_count * dh
    grads, new_rows = pl.pallas_call(
        functools.partial(kernel, dims),
        out_shape=(
            jax.ShapeDtypeStruct((3, tok, width), jnp.bfloat16),
            jax.ShapeDtypeStruct(accum_rows.shape, jnp.float32),
        ),
        in_specs=[resident, resident] + [anywhere] * 4,
        out_specs=(anywhere, anywhere),
        scratch_shapes=[
            pltpu.VMEM((chunks, 4, key_count, heads // chunks * dh), jnp.bfloat16),
            pltpu.VMEM((chunks, 3, span, heads // chunks * dh), jnp.bfloat16),
            pltpu.VMEM(cache_rows.shape, jnp.bfloat16),
            pltpu.VMEM(cache_rows.shape, jnp.float32),
            pltpu.VMEM(accum_rows.shape, jnp.float32),
            pltpu.VMEM(spread, jnp.float32),
            pltpu.VMEM(spread, jnp.float32),
            pltpu.SemaphoreType.DMA((chunks, 2, n)),
            pltpu.SemaphoreType.DMA((chunks, 2, n)),
            pltpu.SemaphoreType.DMA((chunks, n)),
            pltpu.SemaphoreType.DMA((chunks, n)),
            pltpu.SemaphoreType.DMA((chunks, 2)),
            pltpu.SemaphoreType.DMA((4,)),
            pltpu.SMEM((2, 1), jnp.int32),
        ],
        compiler_params=pltpu.CompilerParams(
            collective_id=0, has_side_effects=True, vmem_limit_bytes=56 * 1024 * 1024
        ),
        cost_estimate=pl.CostEstimate(
            flops=10 * pairs, bytes_accessed=16 * accum_rows.size, transcendentals=pairs // dh
        ),
    )(offsets, lengths, by_kind, out_grad[0], cache_rows, accum_rows)
    next_grads = grads.transpose(1, 0, 2)[None]
    return next_grads, new_rows.reshape(past_accum.shape)


def solution(mesh):
    in_specs = (
        P("section", "seq", None, None),
        P("section", "seq", None),
        P("section", None, None, "seq", None),
        P("section", None, None, "seq", None),
        P("section"),
        P("section"),
    )
    out_specs = (P("section", "seq", None, None), P("section", None, None, "seq", None))
    return jax.shard_map(
        functools.partial(per_device, mesh.shape["section"], mesh.shape["seq"]),
        mesh=mesh,
        in_specs=in_specs,
        out_specs=out_specs,
        check_vma=False,
    )
```

```python
import functools
import math

import jax
import jax.numpy as jnp
from jax import lax
from jax.experimental import pallas as pl
from jax.experimental.pallas import tpu as pltpu
from jax.sharding import PartitionSpec as P

DH = 128
MESH = pl.DeviceIdType.MESH
QUERY, KEY, VALUE, DOUT = range(4)
LANES = 128
HIDDEN = -1e30
OVER_LAST = (((1,), (1,)), ((), ()))
OVER_FIRST = (((0,), (0,)), ((), ()))


def score_block(scale, first, start, keys, values, query, dout, length):
    rows = keys.shape[0]
    key_row = lax.broadcasted_iota(jnp.int32, (rows, rows), 0)
    query_row = lax.broadcasted_iota(jnp.int32, (rows, rows), 1)
    seen = (key_row >= first) & (key_row <= query_row) & (key_row + start < length)
    scores = lax.dot_general(keys, query, OVER_LAST, preferred_element_type=jnp.float32) * scale
    dout_row = lax.broadcasted_iota(jnp.int32, dout.shape, 0)
    dout = jnp.where(dout_row + start < length, dout, jnp.zeros_like(dout))
    dprobs = lax.dot_general(values, dout, OVER_LAST, preferred_element_type=jnp.float32)
    return jnp.where(seen, scores, HIDDEN), dprobs, dout


def attention_grads(
    scale, past, keys, values, query, dout, offset, length, start, span_cut, others
):
    key_count, rows = keys.shape[0], query.shape[0]
    key_index = lax.broadcasted_iota(jnp.int32, (key_count, rows), 0)
    query_pos = start + lax.broadcasted_iota(jnp.int32, (key_count, rows), 1)
    in_span = key_index - past
    limit = jnp.where(in_span < 0, offset - past, jnp.minimum(query_pos + 1, span_cut))
    scores = lax.dot_general(keys, query, OVER_LAST, preferred_element_type=jnp.float32) * scale
    masked = jnp.where(in_span < limit, scores, -jnp.inf)
    top = jnp.max(masked, axis=0, keepdims=True)
    if others is not None:
        other_top, other_sum, other_delta = others
        top = jnp.maximum(top, other_top)
        weight = jnp.exp(other_top - top)
    exp_terms = jnp.exp(masked - top)
    total = jnp.sum(exp_terms, axis=0, keepdims=True)
    if others is not None:
        total = total + other_sum * weight
    inverse = 1.0 / total
    attention = exp_terms * inverse
    row_pos = start + lax.broadcasted_iota(jnp.int32, (rows, DH), 0)
    dout = jnp.where(row_pos < length, dout, jnp.zeros_like(dout))
    dprobs = lax.dot_general(values, dout, OVER_LAST, preferred_element_type=jnp.float32)
    delta = jnp.sum(attention * dprobs, axis=0, keepdims=True)
    if others is not None:
        delta = delta + other_delta * weight * inverse
    dscores = (attention * (dprobs - delta)).astype(jnp.bfloat16)
    grad_values = jnp.dot(
        attention.astype(jnp.bfloat16), dout, preferred_element_type=jnp.float32
    )
    grad_keys = jnp.dot(dscores, query, preferred_element_type=jnp.float32) * scale
    grad_query = (
        lax.dot_general(
            dscores, keys, OVER_FIRST, preferred_element_type=jnp.float32
        )
        * scale
    )
    return grad_query, grad_keys, grad_values, (top, inverse, delta)


def kernel(
    dims,
    offset_ref,
    length_ref,
    span_ref,
    dout_ref,
    cache_ref,
    accum_ref,
    grads_ref,
    new_accum_ref,
    held,
    staged,
    cache_low,
    cache_wide,
    accum,
    total_keys,
    total_values,
    send_in,
    recv_in,
    send_out,
    recv_out,
    own_sem,
    io_sem,
    small,
    *pair,
):
    sections, n, heads, tok, past, span, chunks, block = dims
    per_chunk = heads // chunks
    scale = 1.0 / math.sqrt(DH)
    me = lax.axis_index("seq")
    section = lax.axis_index("section")
    before = lax.rem(section + sections - 1, sections)
    after = lax.rem(section + 1, sections)

    load_cache = pltpu.make_async_copy(cache_ref, cache_low, io_sem.at[0])
    load_accum = pltpu.make_async_copy(accum_ref, accum, io_sem.at[1])
    load_offset = pltpu.make_async_copy(offset_ref, small.at[0], io_sem.at[2])
    load_length = pltpu.make_async_copy(length_ref, small.at[1], io_sem.at[3])
    load_cache.start()
    load_accum.start()
    load_offset.start()
    load_length.start()

    last = n - 2
    if pair:
        (far, far_stats, far_final, far_query, far_out, stats, final, mate_send, mate_recv) = pair[:9]
        (far_own, stats_send, stats_recv, final_send, final_recv) = pair[9:14]
        (query_send, query_recv, far_send) = pair[14:]
        in_pair = me >= last
        core = lax.rem(me, 2)
        mate = last + 1 - core
        tail = LANES - 2 * tok

    def peer_at(k):
        half = n // 2
        mine = me // half
        far = (1 - mine) * half + lax.rem(me + k, half)
        near = mine * half + lax.rem(me + k - half + 1, half)
        return jnp.where(k < half, far, near)

    barrier = pltpu.get_barrier_semaphore()

    def greet_peer(k, carry):
        pl.semaphore_signal(barrier, inc=1, device_id=(section, peer_at(k)), device_id_type=MESH)
        return carry

    def greet_sections(k, carry):
        pl.semaphore_signal(barrier, inc=1, device_id=(before, k), device_id_type=MESH)
        pl.semaphore_signal(barrier, inc=1, device_id=(after, k), device_id_type=MESH)
        return carry

    lax.fori_loop(0, n - 1, greet_peer, 0)
    lax.fori_loop(0, n, greet_sections, 0)
    pl.semaphore_wait(barrier, 3 * n - 1)

    def columns(owner, c):
        return pl.ds(pl.multiple_of((owner * heads + c * per_chunk) * DH, DH), per_chunk * DH)

    def span_rows(owner):
        return pl.ds(pl.multiple_of(past + owner * tok, 16), tok)

    def inputs(c, owner, rows):
        cols = columns(owner, c)
        return (
            (span_ref.at[:, :, cols], held.at[c, pl.ds(0, 3), span_rows(rows), :]),
            (dout_ref.at[:, cols], held.at[c, DOUT, span_rows(rows), :]),
        )

    def send_tokens(c, peer):
        return [
            pltpu.make_async_remote_copy(
                src_ref=source,
                dst_ref=target,
                send_sem=send_in.at[c, which, peer],
                recv_sem=recv_in.at[c, which, me],
                device_id=(section, peer),
                device_id_type=MESH,
            )
            for which, (source, target) in enumerate(inputs(c, peer, me))
        ]

    def receive_tokens(c, peer):
        return [
            pltpu.make_async_remote_copy(
                src_ref=source,
                dst_ref=target,
                send_sem=send_in.at[c, which, me],
                recv_sem=recv_in.at[c, which, peer],
                device_id=(section, peer),
                device_id_type=MESH,
            )
            for which, (source, target) in enumerate(inputs(c, me, peer))
        ]

    def own_tokens(c):
        return [
            pltpu.make_async_copy(source, target, own_sem.at[c, which])
            for which, (source, target) in enumerate(inputs(c, me, me))
        ]

    def slim(c, peer, rows, sender):
        cols = columns(peer, c)
        target = held.at[c, QUERY, span_rows(rows), :]
        dout_target = held.at[c, DOUT, span_rows(rows), :]
        return [
            pltpu.make_async_remote_copy(
                src_ref=source,
                dst_ref=destination,
                send_sem=send_in.at[c, which, peer],
                recv_sem=recv_in.at[c, which, rows],
                device_id=(section, sender),
                device_id_type=MESH,
            )
            for which, (source, destination) in enumerate(
                ((span_ref.at[QUERY, :, cols], target), (dout_ref.at[:, cols], dout_target))
            )
        ]

    def each_token_copy(c, peer, outward, act):
        full = send_tokens if outward else receive_tokens
        if not pair:
            for copy in full(c, peer):
                act(copy)
            return
        if outward:
            cut = in_pair & (peer < last)
        else:
            cut = (peer >= last) & (me < last)

        @pl.when(cut)
        def _():
            for copy in slim(c, peer, me, peer) if outward else slim(c, me, peer, peer):
                act(copy)

        @pl.when(jnp.logical_not(cut))
        def _():
            for copy in full(c, peer):
                act(copy)

    def head_columns(owner, c):
        return pl.ds(pl.multiple_of((owner * heads + c * per_chunk + core) * DH, DH), DH)

    def far_inputs(owner):
        rows = pl.ds(pl.multiple_of(tail + (owner - last) * tok, 16), tok)
        cols = pl.ds(0, last * heads * DH)
        return (
            (span_ref.at[:, :, cols], far.at[pl.ds(0, 3), rows, :]),
            (dout_ref.at[:, cols], far.at[DOUT, rows, :]),
        )

    def mate_copies(rows):
        return [
            pltpu.make_async_remote_copy(
                src_ref=source,
                dst_ref=target,
                send_sem=mate_send.at[which],
                recv_sem=mate_recv.at[which],
                device_id=(section, mate),
                device_id_type=MESH,
            )
            for which, (source, target) in enumerate(far_inputs(rows))
        ]

    def own_far():
        return [
            pltpu.make_async_copy(source, target, far_own.at[which])
            for which, (source, target) in enumerate(far_inputs(me))
        ]

    def send_stats(c, owner):
        return pltpu.make_async_remote_copy(
            src_ref=far_stats.at[c, owner],
            dst_ref=stats.at[c, core],
            send_sem=stats_send.at[c, owner],
            recv_sem=stats_recv.at[c, core],
            device_id=(section, owner),
            device_id_type=MESH,
        )

    def receive_stats(c, i):
        return pltpu.make_async_remote_copy(
            src_ref=far_stats.at[c, 0],
            dst_ref=stats.at[c, i],
            send_sem=stats_send.at[c, 0],
            recv_sem=stats_recv.at[c, i],
            device_id=(section, last + i),
            device_id_type=MESH,
        )

    def send_final(c, i, sender, target):
        lanes = pl.ds(i * DH, DH)
        return (
            pltpu.make_async_remote_copy(
                src_ref=final.at[c, i],
                dst_ref=far_final.at[c, sender],
                send_sem=final_send.at[c, i],
                recv_sem=final_recv.at[c, sender],
                device_id=(section, target),
                device_id_type=MESH,
            ),
            pltpu.make_async_remote_copy(
                src_ref=staged.at[c, 0, pl.ds(span - 2 * tok, 2 * tok), lanes],
                dst_ref=far_query.at[c, sender],
                send_sem=query_send.at[c, i],
                recv_sem=query_recv.at[c, sender],
                device_id=(section, target),
                device_id_type=MESH,
            ),
        )

    def send_far(c, owner, i):
        return pltpu.make_async_remote_copy(
            src_ref=far_out.at[c, owner, :, pl.ds(i * tok, tok), :],
            dst_ref=grads_ref.at[:, :, head_columns(owner, c)],
            send_sem=far_send.at[c, owner, i],
            recv_sem=recv_out.at[c, owner],
            device_id=(before, last + i),
            device_id_type=MESH,
        )

    def far_block(c, owner, length):
        lanes = head_columns(owner, c)
        keys, query = far[KEY, :, lanes], far[QUERY, :, lanes]
        masked, dprobs, dout = score_block(
            scale, tail, span - LANES, keys, far[VALUE, :, lanes], query, far[DOUT, :, lanes], length
        )
        return keys, query, masked, dprobs, dout

    def far_scores(length):
        def one(step, carry):
            c, owner = step // last, lax.rem(step, last)
            _, _, masked, dprobs, _ = far_block(c, owner, length)
            top = jnp.max(masked, axis=0, keepdims=True)
            exp_terms = jnp.exp(masked - top)
            far_stats[c, owner, 0:1, :] = top
            far_stats[c, owner, 1:2, :] = jnp.sum(exp_terms, axis=0, keepdims=True)
            far_stats[c, owner, 2:3, :] = jnp.sum(exp_terms * dprobs, axis=0, keepdims=True)
            far_stats[c, owner, 3:8, :] = jnp.zeros((5, LANES), jnp.float32)
            send_stats(c, owner).start()
            return carry

        lax.fori_loop(0, chunks * last, one, 0)

    def far_grads(c, length):
        def one(owner, carry):
            for copy in send_final(c, 0, owner, owner):
                copy.wait_recv()
            keys, query, masked, dprobs, dout = far_block(c, owner, length)
            top = far_final[c, owner, 0:1, :]
            inverse = far_final[c, owner, 1:2, :]
            delta = far_final[c, owner, 2:3, :]
            attention = jnp.exp(masked - top) * inverse
            dscores = (attention * (dprobs - delta)).astype(jnp.bfloat16)
            grad_query = lax.dot_general(
                dscores, keys, OVER_FIRST, preferred_element_type=jnp.float32
            )
            grad_query = grad_query[tail:] * scale + far_query[c, owner].astype(jnp.float32)
            grad_keys = jnp.dot(dscores, query, preferred_element_type=jnp.float32) * scale
            grad_values = jnp.dot(
                attention.astype(jnp.bfloat16), dout, preferred_element_type=jnp.float32
            )
            far_out[c, owner, 0] = grad_query.astype(jnp.bfloat16)
            far_out[c, owner, 1] = grad_keys[tail:].astype(jnp.bfloat16)
            far_out[c, owner, 2] = grad_values[tail:].astype(jnp.bfloat16)
            for i in range(2):
                send_far(c, owner, i).start()
            return carry

        lax.fori_loop(0, last, one, 0)

    def send_grads(c, token_owner):
        rows = pl.ds(pl.multiple_of(token_owner * tok, 16), tok)
        return pltpu.make_async_remote_copy(
            src_ref=staged.at[c, :, rows, :],
            dst_ref=grads_ref.at[:, :, columns(me, c)],
            send_sem=send_out.at[c, token_owner],
            recv_sem=recv_out.at[c, me],
            device_id=(before, token_owner),
            device_id_type=MESH,
        )

    def receive_grads(c, head_owner):
        return pltpu.make_async_remote_copy(
            src_ref=staged.at[c, :, pl.ds(0, tok), :],
            dst_ref=grads_ref.at[:, :, columns(head_owner, c)],
            send_sem=send_out.at[c, head_owner],
            recv_sem=recv_out.at[c, head_owner],
            device_id=(after, head_owner),
            device_id_type=MESH,
        )

    def start_chunk(c, carry):
        def start_peer(k, carry):
            each_token_copy(c, peer_at(k), True, lambda copy: copy.start())
            return carry

        lax.fori_loop(0, n - 1, start_peer, 0)
        for copy in own_tokens(c):
            copy.start()
        return carry

    load_offset.wait()
    load_length.wait()
    offset = small[0, 0]
    length = small[1, 0]
    lead = min(2, chunks)
    if pair:

        @pl.when(in_pair)
        def _():
            for copy in mate_copies(me) + own_far():
                copy.start()

    start_chunk(0, 0)
    if pair:
        edge = pl.ds(past + span - 2 * tok, 2 * tok)

        @pl.when(in_pair)
        def _():
            if tail:
                far[:, pl.ds(0, tail), :] = jnp.zeros((4, tail, far.shape[2]), jnp.bfloat16)
            row = lax.broadcasted_iota(jnp.int32, stats.shape, 2)
            stats[...] = jnp.where(row == 0, HIDDEN, 0.0)
            for copy in own_far():
                copy.wait()
            for copy in mate_copies(mate):
                copy.wait_recv()
            far_scores(length)

        @pl.when(jnp.logical_not(in_pair))
        def _():
            held[:, pl.ds(KEY, 2), edge, :] = jnp.zeros(
                (chunks, 2, 2 * tok, per_chunk * DH), jnp.bfloat16
            )

    lax.fori_loop(1, lead, start_chunk, 0)

    load_cache.wait()
    cache_wide[...] = cache_low[...].astype(jnp.float32)
    for h in range(heads):
        for which in (KEY, VALUE):
            rows = pl.ds((which - KEY) * heads + h, past, stride=2 * heads)
            lanes = pl.ds(h % per_chunk * DH, DH)
            held[h // per_chunk, which, pl.ds(0, past), lanes] = cache_wide[rows, :].astype(jnp.bfloat16)
    load_accum.wait()

    blocks = span // block
    span_cut = length
    if pair:
        span_cut = jnp.where(in_pair, length, jnp.minimum(length, span - 2 * tok))

    def one_head(c, i):
        h = c * per_chunk + i
        lanes = pl.ds(pl.multiple_of(i * DH, DH), DH)
        keys = held[c, KEY, :, lanes]
        values = held[c, VALUE, :, lanes]

        def one_block(start):
            others = None
            if pair:
                ahead = jnp.zeros((1, span - LANES), jnp.float32)
                others = [
                    jnp.concatenate([ahead + fill, stats[c, i, row : row + 1, :]], axis=1)
                    for row, fill in enumerate((HIDDEN, 0.0, 0.0))
                ]
            grad_query, grad_keys, grad_values, ends = attention_grads(
                scale,
                past,
                keys,
                values,
                held[c, QUERY, pl.ds(past + start, block), lanes],
                held[c, DOUT, pl.ds(past + start, block), lanes],
                offset,
                length,
                start,
                span_cut,
                others,
            )
            if pair:
                for row, value in enumerate(ends):
                    final[c, i, row : row + 1, :] = value[:, span - LANES :]
                final[c, i, 3:8, :] = jnp.zeros((5, LANES), jnp.float32)
            staged[c, 0, pl.ds(start, block), lanes] = grad_query.astype(jnp.bfloat16)
            return grad_keys, grad_values

        if blocks == 1:
            grad_keys, grad_values = one_block(0)
        else:
            total_keys[...] = jnp.zeros_like(total_keys)
            total_values[...] = jnp.zeros_like(total_values)

            def step(b, carry):
                more_keys, more_values = one_block(pl.multiple_of(b * block, block))
                total_keys[...] += more_keys
                total_values[...] += more_values
                return carry

            lax.fori_loop(0, blocks, step, 0)
            grad_keys, grad_values = total_keys[...], total_values[...]
        staged[c, 1, :, lanes] = grad_keys[past:].astype(jnp.bfloat16)
        staged[c, 2, :, lanes] = grad_values[past:].astype(jnp.bfloat16)
        accum[pl.ds(h, past, stride=2 * heads), :] += grad_keys[:past]
        accum[pl.ds(heads + h, past, stride=2 * heads), :] += grad_values[:past]

    def work_chunk(c, carry):
        def wait_peer(k, carry):
            each_token_copy(c, peer_at(k), False, lambda copy: copy.wait_recv())
            return carry

        lax.fori_loop(0, n - 1, wait_peer, 0)
        for copy in own_tokens(c):
            copy.wait()

        if pair:

            @pl.when(jnp.logical_not(in_pair))
            def _():
                for i in range(2):
                    receive_stats(c, i).wait_recv()

        def work_head(i, carry):
            one_head(c, i)
            return carry

        lax.fori_loop(0, per_chunk, work_head, 0)

        if pair:

            @pl.when(jnp.logical_not(in_pair))
            def _():
                for i in range(2):
                    for copy in send_final(c, i, me, last + i):
                        copy.start()

        def start_out(k, carry):
            peer = peer_at(k)
            if pair:

                @pl.when(in_pair | (peer < last))
                def _():
                    send_grads(c, peer).start()

            else:
                send_grads(c, peer).start()
            return carry

        lax.fori_loop(0, n - 1, start_out, 0)
        send_grads(c, me).start()

        @pl.when(c + lead < chunks)
        def _():
            start_chunk(c + lead, 0)

        if pair:

            @pl.when(in_pair & (c > 0))
            def _():
                far_grads(c - 1, length)

        return carry

    lax.fori_loop(0, chunks, work_chunk, 0)

    store_accum = pltpu.make_async_copy(accum, new_accum_ref, io_sem.at[1])
    store_accum.start()
    if pair:

        @pl.when(in_pair)
        def _():
            far_grads(chunks - 1, length)
            for copy in mate_copies(me):
                copy.wait_send()

    def finish_chunk(c, carry):
        def sent(k, carry):
            each_token_copy(c, peer_at(k), True, lambda copy: copy.wait_send())
            return carry

        def exchanged(t, carry):
            if pair:

                @pl.when(in_pair | (t < last))
                def _():
                    send_grads(c, t).wait_send()

            else:
                send_grads(c, t).wait_send()
            receive_grads(c, t).wait_recv()
            return carry

        lax.fori_loop(0, n - 1, sent, 0)
        lax.fori_loop(0, n, exchanged, 0)
        if pair:

            @pl.when(jnp.logical_not(in_pair))
            def _():
                for i in range(2):
                    for copy in send_final(c, i, me, last + i):
                        copy.wait_send()

            @pl.when(in_pair)
            def _():
                def far_sent(owner, carry):
                    send_stats(c, owner).wait_send()
                    for i in range(2):
                        send_far(c, owner, i).wait_send()
                    return carry

                lax.fori_loop(0, last, far_sent, 0)

        return carry

    lax.fori_loop(0, chunks, finish_chunk, 0)
    store_accum.wait()


def per_device(sections, n, span_inputs, out_grad, past_cache, past_accum, offsets, lengths):
    _, tok, _, width = span_inputs.shape
    _, past, _, heads, dh = past_cache.shape
    span = tok * n
    key_count = past + span
    chunks = 4 if heads % 4 == 0 else 1
    block = min(span, 256 if key_count <= 1024 else 128)
    by_kind = span_inputs[0].transpose(1, 0, 2)
    cache_rows = past_cache.reshape(past * 2 * heads, dh)
    accum_rows = past_accum.reshape(past * 2 * heads, dh)
    dims = (sections, n, heads, tok, past, span, chunks, block)
    spread = (key_count, dh) if span > block else (8, dh)
    anywhere = pl.BlockSpec(memory_space=pl.ANY)
    resident = pl.BlockSpec(memory_space=pltpu.HBM)
    pair_scratch = []
    if heads // chunks == 2 and 2 * tok <= LANES <= span == block and n > 2 and n % 2 == 0:
        last = n - 2
        dma = pltpu.SemaphoreType.DMA
        pair_scratch = [
            pltpu.VMEM((4, LANES, last * heads * dh), jnp.bfloat16),
            pltpu.VMEM((chunks, last, 8, LANES), jnp.float32),
            pltpu.VMEM((chunks, last, 8, LANES), jnp.float32),
            pltpu.VMEM((chunks, last, 2 * tok, dh), jnp.bfloat16),
            pltpu.VMEM((chunks, last, 3, 2 * tok, dh), jnp.bfloat16),
            pltpu.VMEM((chunks, 2, 8, LANES), jnp.float32),
            pltpu.VMEM((chunks, 2, 8, LANES), jnp.float32),
            dma((2,)),
            dma((2,)),
            dma((2,)),
            dma((chunks, last)),
            dma((chunks, 2)),
            dma((chunks, 2)),
            dma((chunks, last)),
            dma((chunks, 2)),
            dma((chunks, last)),
            dma((chunks, last, 2)),
        ]
    pairs = heads * span * key_count * dh
    grads, new_rows = pl.pallas_call(
        functools.partial(kernel, dims),
        out_shape=(
            jax.ShapeDtypeStruct((3, tok, width), jnp.bfloat16),
            jax.ShapeDtypeStruct(accum_rows.shape, jnp.float32),
        ),
        in_specs=[resident, resident] + [anywhere] * 4,
        out_specs=(anywhere, anywhere),
        scratch_shapes=[
            pltpu.VMEM((chunks, 4, key_count, heads // chunks * dh), jnp.bfloat16),
            pltpu.VMEM((chunks, 3, span, heads // chunks * dh), jnp.bfloat16),
            pltpu.VMEM(cache_rows.shape, jnp.bfloat16),
            pltpu.VMEM(cache_rows.shape, jnp.float32),
            pltpu.VMEM(accum_rows.shape, jnp.float32),
            pltpu.VMEM(spread, jnp.float32),
            pltpu.VMEM(spread, jnp.float32),
            pltpu.SemaphoreType.DMA((chunks, 2, n)),
            pltpu.SemaphoreType.DMA((chunks, 2, n)),
            pltpu.SemaphoreType.DMA((chunks, n)),
            pltpu.SemaphoreType.DMA((chunks, n)),
            pltpu.SemaphoreType.DMA((chunks, 2)),
            pltpu.SemaphoreType.DMA((4,)),
            pltpu.SMEM((2, 1), jnp.int32),
            *pair_scratch,
        ],
        compiler_params=pltpu.CompilerParams(
            collective_id=0, has_side_effects=True, vmem_limit_bytes=56 * 1024 * 1024
        ),
        cost_estimate=pl.CostEstimate(
            flops=10 * pairs, bytes_accessed=16 * accum_rows.size, transcendentals=pairs // dh
        ),
    )(offsets, lengths, by_kind, out_grad[0], cache_rows, accum_rows)
    next_grads = grads.transpose(1, 0, 2)[None]
    return next_grads, new_rows.reshape(past_accum.shape)


def solution(mesh):
    in_specs = (
        P("section", "seq", None, None),
        P("section", "seq", None),
        P("section", None, None, "seq", None),
        P("section", None, None, "seq", None),
        P("section"),
        P("section"),
    )
    out_specs = (P("section", "seq", None, None), P("section", None, None, "seq", None))
    return jax.shard_map(
        functools.partial(per_device, mesh.shape["section"], mesh.shape["seq"]),
        mesh=mesh,
        in_specs=in_specs,
        out_specs=out_specs,
        check_vma=False,
    )
```

```python
import functools
import math

import jax
import jax.numpy as jnp
from jax import lax
from jax.experimental import pallas as pl
from jax.experimental.pallas import tpu as pltpu
from jax.sharding import PartitionSpec as P

DH = 128
MESH = pl.DeviceIdType.MESH
QUERY, KEY, VALUE, DOUT = range(4)
LANES = 128
HIDDEN = -1e30
OVER_LAST = (((1,), (1,)), ((), ()))
OVER_FIRST = (((0,), (0,)), ((), ()))


def score_block(scale, first, start, keys, values, query, dout, length):
    rows = keys.shape[0]
    key_row = lax.broadcasted_iota(jnp.int32, (rows, rows), 0)
    query_row = lax.broadcasted_iota(jnp.int32, (rows, rows), 1)
    seen = (key_row >= first) & (key_row <= query_row) & (key_row + start < length)
    scores = lax.dot_general(keys, query, OVER_LAST, preferred_element_type=jnp.float32) * scale
    dout_row = lax.broadcasted_iota(jnp.int32, dout.shape, 0)
    dout = jnp.where(dout_row + start < length, dout, jnp.zeros_like(dout))
    dprobs = lax.dot_general(values, dout, OVER_LAST, preferred_element_type=jnp.float32)
    return jnp.where(seen, scores, HIDDEN), dprobs, dout


def attention_grads(
    scale, past, keys, values, query, dout, offset, length, start, span_cut, others
):
    key_count, rows = keys.shape[0], query.shape[0]
    key_index = lax.broadcasted_iota(jnp.int32, (key_count, rows), 0)
    query_pos = start + lax.broadcasted_iota(jnp.int32, (key_count, rows), 1)
    in_span = key_index - past
    limit = jnp.where(in_span < 0, offset - past, jnp.minimum(query_pos + 1, span_cut))
    scores = lax.dot_general(keys, query, OVER_LAST, preferred_element_type=jnp.float32) * scale
    masked = jnp.where(in_span < limit, scores, -jnp.inf)
    top = jnp.max(masked, axis=0, keepdims=True)
    if others is not None:
        other_top, other_sum, other_delta = others
        top = jnp.maximum(top, other_top)
        weight = jnp.exp(other_top - top)
    exp_terms = jnp.exp(masked - top)
    total = jnp.sum(exp_terms, axis=0, keepdims=True)
    if others is not None:
        total = total + other_sum * weight
    inverse = 1.0 / total
    attention = exp_terms * inverse
    row_pos = start + lax.broadcasted_iota(jnp.int32, (rows, DH), 0)
    dout = jnp.where(row_pos < length, dout, jnp.zeros_like(dout))
    dprobs = lax.dot_general(values, dout, OVER_LAST, preferred_element_type=jnp.float32)
    delta = jnp.sum(attention * dprobs, axis=0, keepdims=True)
    if others is not None:
        delta = delta + other_delta * weight * inverse
    dscores = (attention * (dprobs - delta)).astype(jnp.bfloat16)
    grad_values = jnp.dot(
        attention.astype(jnp.bfloat16), dout, preferred_element_type=jnp.float32
    )
    grad_keys = jnp.dot(dscores, query, preferred_element_type=jnp.float32) * scale
    grad_query = (
        lax.dot_general(
            dscores, keys, OVER_FIRST, preferred_element_type=jnp.float32
        )
        * scale
    )
    return grad_query, grad_keys, grad_values, (top, inverse, delta)


def kernel(
    dims,
    offset_ref,
    length_ref,
    span_ref,
    dout_ref,
    cache_ref,
    accum_ref,
    grads_ref,
    new_accum_ref,
    held,
    staged,
    cache_low,
    cache_wide,
    accum,
    total_keys,
    total_values,
    send_in,
    recv_in,
    send_out,
    recv_out,
    own_sem,
    io_sem,
    small,
    *pair,
):
    sections, n, heads, tok, past, span, chunks, block = dims
    per_chunk = heads // chunks
    scale = 1.0 / math.sqrt(DH)
    me = lax.axis_index("seq")
    section = lax.axis_index("section")
    before = lax.rem(section + sections - 1, sections)
    after = lax.rem(section + 1, sections)

    load_cache = pltpu.make_async_copy(cache_ref, cache_low, io_sem.at[0])
    load_accum = pltpu.make_async_copy(accum_ref, accum, io_sem.at[1])
    load_offset = pltpu.make_async_copy(offset_ref, small.at[0], io_sem.at[2])
    load_length = pltpu.make_async_copy(length_ref, small.at[1], io_sem.at[3])
    load_cache.start()
    load_accum.start()
    load_offset.start()
    load_length.start()

    last = n - 2
    if pair:
        (far, far_stats, far_final, far_query, far_out, stats, final, mate_send, mate_recv) = pair[:9]
        (far_own, stats_send, stats_recv, final_send, final_recv) = pair[9:14]
        (query_send, query_recv, far_send) = pair[14:]
        in_pair = me >= last
        core = lax.rem(me, 2)
        mate = last + 1 - core
        tail = LANES - 2 * tok

    def peer_at(k):
        half = n // 2
        mine = me // half
        far = (1 - mine) * half + lax.rem(me + k, half)
        near = mine * half + lax.rem(me + k - half + 1, half)
        return jnp.where(k < half, far, near)

    barrier = pltpu.get_barrier_semaphore()

    def greet_peer(k, carry):
        pl.semaphore_signal(barrier, inc=1, device_id=(section, peer_at(k)), device_id_type=MESH)
        return carry

    def greet_sections(k, carry):
        pl.semaphore_signal(barrier, inc=1, device_id=(before, k), device_id_type=MESH)
        pl.semaphore_signal(barrier, inc=1, device_id=(after, k), device_id_type=MESH)
        return carry

    lax.fori_loop(0, n - 1, greet_peer, 0)
    lax.fori_loop(0, n, greet_sections, 0)
    pl.semaphore_wait(barrier, 3 * n - 1)

    def columns(owner, c):
        return pl.ds(pl.multiple_of((owner * heads + c * per_chunk) * DH, DH), per_chunk * DH)

    def span_rows(owner):
        return pl.ds(pl.multiple_of(past + owner * tok, 16), tok)

    def inputs(c, owner, rows):
        cols = columns(owner, c)
        return (
            (span_ref.at[:, :, cols], held.at[c, pl.ds(0, 3), span_rows(rows), :]),
            (dout_ref.at[:, cols], held.at[c, DOUT, span_rows(rows), :]),
        )

    def send_tokens(c, peer):
        return [
            pltpu.make_async_remote_copy(
                src_ref=source,
                dst_ref=target,
                send_sem=send_in.at[c, which, peer],
                recv_sem=recv_in.at[c, which, me],
                device_id=(section, peer),
                device_id_type=MESH,
            )
            for which, (source, target) in enumerate(inputs(c, peer, me))
        ]

    def receive_tokens(c, peer):
        return [
            pltpu.make_async_remote_copy(
                src_ref=source,
                dst_ref=target,
                send_sem=send_in.at[c, which, me],
                recv_sem=recv_in.at[c, which, peer],
                device_id=(section, peer),
                device_id_type=MESH,
            )
            for which, (source, target) in enumerate(inputs(c, me, peer))
        ]

    def own_tokens(c):
        return [
            pltpu.make_async_copy(source, target, own_sem.at[c, which])
            for which, (source, target) in enumerate(inputs(c, me, me))
        ]

    def slim(c, peer, rows, sender):
        cols = columns(peer, c)
        target = held.at[c, QUERY, span_rows(rows), :]
        dout_target = held.at[c, DOUT, span_rows(rows), :]
        return [
            pltpu.make_async_remote_copy(
                src_ref=source,
                dst_ref=destination,
                send_sem=send_in.at[c, which, peer],
                recv_sem=recv_in.at[c, which, rows],
                device_id=(section, sender),
                device_id_type=MESH,
            )
            for which, (source, destination) in enumerate(
                ((span_ref.at[QUERY, :, cols], target), (dout_ref.at[:, cols], dout_target))
            )
        ]

    def each_token_copy(c, peer, outward, act):
        full = send_tokens if outward else receive_tokens
        if not pair:
            for copy in full(c, peer):
                act(copy)
            return
        if outward:
            cut = in_pair & (peer < last)
        else:
            cut = (peer >= last) & (me < last)

        @pl.when(cut)
        def _():
            for copy in slim(c, peer, me, peer) if outward else slim(c, me, peer, peer):
                act(copy)

        @pl.when(jnp.logical_not(cut))
        def _():
            for copy in full(c, peer):
                act(copy)

    def head_columns(owner, c):
        return pl.ds(pl.multiple_of((owner * heads + c * per_chunk + core) * DH, DH), DH)

    def far_inputs(owner):
        rows = pl.ds(pl.multiple_of(tail + (owner - last) * tok, 16), tok)
        cols = pl.ds(0, last * heads * DH)
        return (
            (span_ref.at[:, :, cols], far.at[pl.ds(0, 3), rows, :]),
            (dout_ref.at[:, cols], far.at[DOUT, rows, :]),
        )

    def mate_copies(rows):
        return [
            pltpu.make_async_remote_copy(
                src_ref=source,
                dst_ref=target,
                send_sem=mate_send.at[which],
                recv_sem=mate_recv.at[which],
                device_id=(section, mate),
                device_id_type=MESH,
            )
            for which, (source, target) in enumerate(far_inputs(rows))
        ]

    def own_far():
        return [
            pltpu.make_async_copy(source, target, far_own.at[which])
            for which, (source, target) in enumerate(far_inputs(me))
        ]

    def send_stats(c, owner):
        return pltpu.make_async_remote_copy(
            src_ref=far_stats.at[c, owner],
            dst_ref=stats.at[c, core],
            send_sem=stats_send.at[c, owner],
            recv_sem=stats_recv.at[c, core],
            device_id=(section, owner),
            device_id_type=MESH,
        )

    def receive_stats(c, i):
        return pltpu.make_async_remote_copy(
            src_ref=far_stats.at[c, 0],
            dst_ref=stats.at[c, i],
            send_sem=stats_send.at[c, 0],
            recv_sem=stats_recv.at[c, i],
            device_id=(section, last + i),
            device_id_type=MESH,
        )

    def send_final(c, i, sender, target):
        lanes = pl.ds(i * DH, DH)
        return (
            pltpu.make_async_remote_copy(
                src_ref=final.at[c, i],
                dst_ref=far_final.at[c, sender],
                send_sem=final_send.at[c, i],
                recv_sem=final_recv.at[c, sender],
                device_id=(section, target),
                device_id_type=MESH,
            ),
            pltpu.make_async_remote_copy(
                src_ref=staged.at[c, 0, pl.ds(span - 2 * tok, 2 * tok), lanes],
                dst_ref=far_query.at[c, sender],
                send_sem=query_send.at[c, i],
                recv_sem=query_recv.at[c, sender],
                device_id=(section, target),
                device_id_type=MESH,
            ),
        )

    def send_far(c, owner, i):
        return pltpu.make_async_remote_copy(
            src_ref=far_out.at[c, owner, :, pl.ds(i * tok, tok), :],
            dst_ref=grads_ref.at[:, :, head_columns(owner, c)],
            send_sem=far_send.at[c, owner, i],
            recv_sem=recv_out.at[c, owner],
            device_id=(before, last + i),
            device_id_type=MESH,
        )

    def far_block(c, owner, length):
        lanes = head_columns(owner, c)
        keys, query = far[KEY, :, lanes], far[QUERY, :, lanes]
        masked, dprobs, dout = score_block(
            scale, tail, span - LANES, keys, far[VALUE, :, lanes], query, far[DOUT, :, lanes], length
        )
        return keys, query, masked, dprobs, dout

    def far_scores(length):
        def one(c, carry):
            found = []
            for owner in range(last):
                _, _, masked, dprobs, _ = far_block(c, owner, length)
                top = jnp.max(masked, axis=0, keepdims=True)
                exp_terms = jnp.exp(masked - top)
                total = jnp.sum(exp_terms, axis=0, keepdims=True)
                found.append((top, total, jnp.sum(exp_terms * dprobs, axis=0, keepdims=True)))
            for owner in range(last):
                for row in range(3):
                    far_stats[c, owner, row : row + 1, :] = found[owner][row]
                far_stats[c, owner, 3:8, :] = jnp.zeros((5, LANES), jnp.float32)
            for owner in range(last):
                send_stats(c, owner).start()
            return carry

        lax.fori_loop(0, chunks, one, 0)

    def far_grads(c, length):
        for owner in range(last):
            for copy in send_final(c, 0, owner, owner):
                copy.wait_recv()
        found = []
        for owner in range(last):
            keys, query, masked, dprobs, dout = far_block(c, owner, length)
            top = far_final[c, owner, 0:1, :]
            inverse = far_final[c, owner, 1:2, :]
            delta = far_final[c, owner, 2:3, :]
            attention = jnp.exp(masked - top) * inverse
            dscores = (attention * (dprobs - delta)).astype(jnp.bfloat16)
            grad_query = lax.dot_general(
                dscores, keys, OVER_FIRST, preferred_element_type=jnp.float32
            )
            grad_query = grad_query[tail:] * scale + far_query[c, owner].astype(jnp.float32)
            grad_keys = jnp.dot(dscores, query, preferred_element_type=jnp.float32) * scale
            grad_values = jnp.dot(
                attention.astype(jnp.bfloat16), dout, preferred_element_type=jnp.float32
            )
            found.append((grad_query, grad_keys[tail:], grad_values[tail:]))
        for owner in range(last):
            for kind in range(3):
                far_out[c, owner, kind] = found[owner][kind].astype(jnp.bfloat16)
        for owner in range(last):
            for i in range(2):
                send_far(c, owner, i).start()

    def send_grads(c, token_owner):
        rows = pl.ds(pl.multiple_of(token_owner * tok, 16), tok)
        return pltpu.make_async_remote_copy(
            src_ref=staged.at[c, :, rows, :],
            dst_ref=grads_ref.at[:, :, columns(me, c)],
            send_sem=send_out.at[c, token_owner],
            recv_sem=recv_out.at[c, me],
            device_id=(before, token_owner),
            device_id_type=MESH,
        )

    def receive_grads(c, head_owner):
        return pltpu.make_async_remote_copy(
            src_ref=staged.at[c, :, pl.ds(0, tok), :],
            dst_ref=grads_ref.at[:, :, columns(head_owner, c)],
            send_sem=send_out.at[c, head_owner],
            recv_sem=recv_out.at[c, head_owner],
            device_id=(after, head_owner),
            device_id_type=MESH,
        )

    def start_chunk(c, carry):
        def start_peer(k, carry):
            each_token_copy(c, peer_at(k), True, lambda copy: copy.start())
            return carry

        lax.fori_loop(0, n - 1, start_peer, 0)
        for copy in own_tokens(c):
            copy.start()
        return carry

    load_offset.wait()
    load_length.wait()
    offset = small[0, 0]
    length = small[1, 0]
    lead = min(2, chunks)
    if pair:

        @pl.when(in_pair)
        def _():
            for copy in mate_copies(me) + own_far():
                copy.start()

    lax.fori_loop(0, lead, start_chunk, 0)
    if pair:
        edge = pl.ds(past + span - 2 * tok, 2 * tok)

        @pl.when(in_pair)
        def _():
            if tail:
                far[:, pl.ds(0, tail), :] = jnp.zeros((4, tail, far.shape[2]), jnp.bfloat16)
            row = lax.broadcasted_iota(jnp.int32, stats.shape, 2)
            stats[...] = jnp.where(row == 0, HIDDEN, 0.0)
            for copy in own_far():
                copy.wait()
            for copy in mate_copies(mate):
                copy.wait_recv()
            far_scores(length)

        @pl.when(jnp.logical_not(in_pair))
        def _():
            held[:, pl.ds(KEY, 2), edge, :] = jnp.zeros(
                (chunks, 2, 2 * tok, per_chunk * DH), jnp.bfloat16
            )


    load_cache.wait()
    cache_wide[...] = cache_low[...].astype(jnp.float32)
    for h in range(heads):
        for which in (KEY, VALUE):
            rows = pl.ds((which - KEY) * heads + h, past, stride=2 * heads)
            lanes = pl.ds(h % per_chunk * DH, DH)
            held[h // per_chunk, which, pl.ds(0, past), lanes] = cache_wide[rows, :].astype(jnp.bfloat16)
    load_accum.wait()

    blocks = span // block
    span_cut = length
    if pair:
        span_cut = jnp.where(in_pair, length, jnp.minimum(length, span - 2 * tok))

    def one_head(c, i):
        h = c * per_chunk + i
        lanes = pl.ds(i * DH, DH)
        keys = held[c, KEY, :, lanes]
        values = held[c, VALUE, :, lanes]

        def one_block(start):
            others = None
            if pair:
                ahead = jnp.zeros((1, span - LANES), jnp.float32)
                others = [
                    jnp.concatenate([ahead + fill, stats[c, i, row : row + 1, :]], axis=1)
                    for row, fill in enumerate((HIDDEN, 0.0, 0.0))
                ]
            grad_query, grad_keys, grad_values, ends = attention_grads(
                scale,
                past,
                keys,
                values,
                held[c, QUERY, pl.ds(past + start, block), lanes],
                held[c, DOUT, pl.ds(past + start, block), lanes],
                offset,
                length,
                start,
                span_cut,
                others,
            )
            if pair:
                for row, value in enumerate(ends):
                    final[c, i, row : row + 1, :] = value[:, span - LANES :]
                final[c, i, 3:8, :] = jnp.zeros((5, LANES), jnp.float32)
            staged[c, 0, pl.ds(start, block), lanes] = grad_query.astype(jnp.bfloat16)
            return grad_keys, grad_values

        if blocks == 1:
            grad_keys, grad_values = one_block(0)
        else:
            total_keys[...] = jnp.zeros_like(total_keys)
            total_values[...] = jnp.zeros_like(total_values)

            def step(b, carry):
                more_keys, more_values = one_block(pl.multiple_of(b * block, block))
                total_keys[...] += more_keys
                total_values[...] += more_values
                return carry

            lax.fori_loop(0, blocks, step, 0)
            grad_keys, grad_values = total_keys[...], total_values[...]
        staged[c, 1, :, lanes] = grad_keys[past:].astype(jnp.bfloat16)
        staged[c, 2, :, lanes] = grad_values[past:].astype(jnp.bfloat16)
        accum[pl.ds(h, past, stride=2 * heads), :] += grad_keys[:past]
        accum[pl.ds(heads + h, past, stride=2 * heads), :] += grad_values[:past]

    def work_chunk(c, carry):
        def wait_peer(k, carry):
            each_token_copy(c, peer_at(k), False, lambda copy: copy.wait_recv())
            return carry

        lax.fori_loop(0, n - 1, wait_peer, 0)
        for copy in own_tokens(c):
            copy.wait()

        @pl.when(c + lead < chunks)
        def _():
            start_chunk(c + lead, 0)

        if pair:

            @pl.when(jnp.logical_not(in_pair))
            def _():
                for i in range(2):
                    receive_stats(c, i).wait_recv()

        for i in range(per_chunk):
            one_head(c, i)

        if pair:

            @pl.when(jnp.logical_not(in_pair))
            def _():
                for i in range(2):
                    for copy in send_final(c, i, me, last + i):
                        copy.start()

        def start_out(k, carry):
            peer = peer_at(k)
            if pair:

                @pl.when(in_pair | (peer < last))
                def _():
                    send_grads(c, peer).start()

            else:
                send_grads(c, peer).start()
            return carry

        lax.fori_loop(0, n - 1, start_out, 0)
        send_grads(c, me).start()

        if pair:

            @pl.when(in_pair & (c > 0))
            def _():
                far_grads(c - 1, length)

        return carry

    lax.fori_loop(0, chunks, work_chunk, 0)

    store_accum = pltpu.make_async_copy(accum, new_accum_ref, io_sem.at[1])
    store_accum.start()
    if pair:

        @pl.when(in_pair)
        def _():
            far_grads(chunks - 1, length)
            for copy in mate_copies(me):
                copy.wait_send()

    def finish_chunk(c, carry):
        def sent(k, carry):
            each_token_copy(c, peer_at(k), True, lambda copy: copy.wait_send())
            return carry

        def exchanged(t, carry):
            if pair:

                @pl.when(in_pair | (t < last))
                def _():
                    send_grads(c, t).wait_send()

            else:
                send_grads(c, t).wait_send()
            receive_grads(c, t).wait_recv()
            return carry

        lax.fori_loop(0, n - 1, sent, 0)
        lax.fori_loop(0, n, exchanged, 0)
        if pair:

            @pl.when(jnp.logical_not(in_pair))
            def _():
                for i in range(2):
                    for copy in send_final(c, i, me, last + i):
                        copy.wait_send()

            @pl.when(in_pair)
            def _():
                def far_sent(owner, carry):
                    send_stats(c, owner).wait_send()
                    for i in range(2):
                        send_far(c, owner, i).wait_send()
                    return carry

                lax.fori_loop(0, last, far_sent, 0)

        return carry

    lax.fori_loop(0, chunks, finish_chunk, 0)
    store_accum.wait()


def per_device(sections, n, span_inputs, out_grad, past_cache, past_accum, offsets, lengths):
    _, tok, _, width = span_inputs.shape
    _, past, _, heads, dh = past_cache.shape
    span = tok * n
    key_count = past + span
    chunks = 4 if heads % 4 == 0 else 1
    block = min(span, 256 if key_count <= 1024 else 128)
    by_kind = span_inputs[0].transpose(1, 0, 2)
    cache_rows = past_cache.reshape(past * 2 * heads, dh)
    accum_rows = past_accum.reshape(past * 2 * heads, dh)
    dims = (sections, n, heads, tok, past, span, chunks, block)
    spread = (key_count, dh) if span > block else (8, dh)
    anywhere = pl.BlockSpec(memory_space=pl.ANY)
    resident = pl.BlockSpec(memory_space=pltpu.HBM)
    pair_scratch = []
    if heads // chunks == 2 and 2 * tok <= LANES <= span == block and n > 2 and n % 2 == 0:
        last = n - 2
        dma = pltpu.SemaphoreType.DMA
        pair_scratch = [
            pltpu.VMEM((4, LANES, last * heads * dh), jnp.bfloat16),
            pltpu.VMEM((chunks, last, 8, LANES), jnp.float32),
            pltpu.VMEM((chunks, last, 8, LANES), jnp.float32),
            pltpu.VMEM((chunks, last, 2 * tok, dh), jnp.bfloat16),
            pltpu.VMEM((chunks, last, 3, 2 * tok, dh), jnp.bfloat16),
            pltpu.VMEM((chunks, 2, 8, LANES), jnp.float32),
            pltpu.VMEM((chunks, 2, 8, LANES), jnp.float32),
            dma((2,)),
            dma((2,)),
            dma((2,)),
            dma((chunks, last)),
            dma((chunks, 2)),
            dma((chunks, 2)),
            dma((chunks, last)),
            dma((chunks, 2)),
            dma((chunks, last)),
            dma((chunks, last, 2)),
        ]
    pairs = heads * span * key_count * dh
    grads, new_rows = pl.pallas_call(
        functools.partial(kernel, dims),
        out_shape=(
            jax.ShapeDtypeStruct((3, tok, width), jnp.bfloat16),
            jax.ShapeDtypeStruct(accum_rows.shape, jnp.float32),
        ),
        in_specs=[resident, resident] + [anywhere] * 4,
        out_specs=(anywhere, anywhere),
        scratch_shapes=[
            pltpu.VMEM((chunks, 4, key_count, heads // chunks * dh), jnp.bfloat16),
            pltpu.VMEM((chunks, 3, span, heads // chunks * dh), jnp.bfloat16),
            pltpu.VMEM(cache_rows.shape, jnp.bfloat16),
            pltpu.VMEM(cache_rows.shape, jnp.float32),
            pltpu.VMEM(accum_rows.shape, jnp.float32),
            pltpu.VMEM(spread, jnp.float32),
            pltpu.VMEM(spread, jnp.float32),
            pltpu.SemaphoreType.DMA((chunks, 2, n)),
            pltpu.SemaphoreType.DMA((chunks, 2, n)),
            pltpu.SemaphoreType.DMA((chunks, n)),
            pltpu.SemaphoreType.DMA((chunks, n)),
            pltpu.SemaphoreType.DMA((chunks, 2)),
            pltpu.SemaphoreType.DMA((4,)),
            pltpu.SMEM((2, 1), jnp.int32),
            *pair_scratch,
        ],
        compiler_params=pltpu.CompilerParams(
            collective_id=0, has_side_effects=True, vmem_limit_bytes=56 * 1024 * 1024
        ),
        cost_estimate=pl.CostEstimate(
            flops=10 * pairs, bytes_accessed=16 * accum_rows.size, transcendentals=pairs // dh
        ),
    )(offsets, lengths, by_kind, out_grad[0], cache_rows, accum_rows)
    next_grads = grads.transpose(1, 0, 2)[None]
    return next_grads, new_rows.reshape(past_accum.shape)


def solution(mesh):
    in_specs = (
        P("section", "seq", None, None),
        P("section", "seq", None),
        P("section", None, None, "seq", None),
        P("section", None, None, "seq", None),
        P("section"),
        P("section"),
    )
    out_specs = (P("section", "seq", None, None), P("section", None, None, "seq", None))
    return jax.shard_map(
        functools.partial(per_device, mesh.shape["section"], mesh.shape["seq"]),
        mesh=mesh,
        in_specs=in_specs,
        out_specs=out_specs,
        check_vma=False,
    )
```

```python
import functools
import math

import jax
import jax.numpy as jnp
from jax import lax
from jax.experimental import pallas as pl
from jax.experimental.pallas import tpu as pltpu
from jax.sharding import PartitionSpec as P

DH = 128
MESH = pl.DeviceIdType.MESH
QUERY, KEY, VALUE, DOUT = range(4)
LANES = 128
HIDDEN = -1e30
OVER_LAST = (((1,), (1,)), ((), ()))
OVER_FIRST = (((0,), (0,)), ((), ()))


def score_block(scale, first, start, keys, values, query, dout, length):
    rows = keys.shape[0]
    key_row = lax.broadcasted_iota(jnp.int32, (rows, rows), 0)
    query_row = lax.broadcasted_iota(jnp.int32, (rows, rows), 1)
    seen = (key_row >= first) & (key_row <= query_row) & (key_row + start < length)
    scores = lax.dot_general(keys, query, OVER_LAST, preferred_element_type=jnp.float32) * scale
    dout_row = lax.broadcasted_iota(jnp.int32, dout.shape, 0)
    dout = jnp.where(dout_row + start < length, dout, jnp.zeros_like(dout))
    dprobs = lax.dot_general(values, dout, OVER_LAST, preferred_element_type=jnp.float32)
    return jnp.where(seen, scores, HIDDEN), dprobs, dout


def attention_grads(
    scale, past, keys, values, query, dout, offset, length, start, span_cut, others
):
    key_count, rows = keys.shape[0], query.shape[0]
    key_index = lax.broadcasted_iota(jnp.int32, (key_count, rows), 0)
    query_pos = start + lax.broadcasted_iota(jnp.int32, (key_count, rows), 1)
    in_span = key_index - past
    limit = jnp.where(in_span < 0, offset - past, jnp.minimum(query_pos + 1, span_cut))
    scores = lax.dot_general(keys, query, OVER_LAST, preferred_element_type=jnp.float32) * scale
    masked = jnp.where(in_span < limit, scores, -jnp.inf)
    top = jnp.max(masked, axis=0, keepdims=True)
    if others is not None:
        other_top, other_sum, other_delta = others
        top = jnp.maximum(top, other_top)
        weight = jnp.exp(other_top - top)
    exp_terms = jnp.exp(masked - top)
    total = jnp.sum(exp_terms, axis=0, keepdims=True)
    if others is not None:
        total = total + other_sum * weight
    inverse = 1.0 / total
    attention = exp_terms * inverse
    row_pos = start + lax.broadcasted_iota(jnp.int32, (rows, DH), 0)
    dout = jnp.where(row_pos < length, dout, jnp.zeros_like(dout))
    dprobs = lax.dot_general(values, dout, OVER_LAST, preferred_element_type=jnp.float32)
    delta = jnp.sum(attention * dprobs, axis=0, keepdims=True)
    if others is not None:
        delta = delta + other_delta * weight * inverse
    dscores = (attention * (dprobs - delta)).astype(jnp.bfloat16)
    grad_values = jnp.dot(
        attention.astype(jnp.bfloat16), dout, preferred_element_type=jnp.float32
    )
    grad_keys = jnp.dot(dscores, query, preferred_element_type=jnp.float32) * scale
    grad_query = (
        lax.dot_general(
            dscores, keys, OVER_FIRST, preferred_element_type=jnp.float32
        )
        * scale
    )
    return grad_query, grad_keys, grad_values, (top, inverse, delta)


def kernel(
    dims,
    offset_ref,
    length_ref,
    span_ref,
    dout_ref,
    cache_ref,
    accum_ref,
    grads_ref,
    new_accum_ref,
    held,
    staged,
    cache_low,
    cache_wide,
    accum,
    total_keys,
    total_values,
    send_in,
    recv_in,
    send_out,
    recv_out,
    own_sem,
    io_sem,
    small,
    *pair,
):
    sections, n, heads, tok, past, span, chunks, block = dims
    per_chunk = heads // chunks
    scale = 1.0 / math.sqrt(DH)
    me = lax.axis_index("seq")
    section = lax.axis_index("section")
    before = lax.rem(section + sections - 1, sections)
    after = lax.rem(section + 1, sections)

    load_cache = pltpu.make_async_copy(cache_ref, cache_low, io_sem.at[0])
    load_accum = pltpu.make_async_copy(accum_ref, accum, io_sem.at[1])
    load_offset = pltpu.make_async_copy(offset_ref, small.at[0], io_sem.at[2])
    load_length = pltpu.make_async_copy(length_ref, small.at[1], io_sem.at[3])
    load_cache.start()
    load_accum.start()
    load_offset.start()
    load_length.start()

    last = n - 2
    if pair:
        (far, far_stats, far_final, far_query, far_out, stats, final, mate_send, mate_recv) = pair[:9]
        (far_own, stats_send, stats_recv, final_send, final_recv) = pair[9:14]
        (query_send, query_recv, far_send, relay, relay_send, relay_recv) = pair[14:]
        in_pair = me >= last
        core = lax.rem(me, 2)
        mate = last + 1 - core
        tail = LANES - 2 * tok

    def peer_at(k):
        half = n // 2
        mine = me // half
        far = (1 - mine) * half + lax.rem(me + k, half)
        near = mine * half + lax.rem(me + k - half + 1, half)
        return jnp.where(k < half, far, near)

    barrier = pltpu.get_barrier_semaphore()

    def greet_peer(k, carry):
        pl.semaphore_signal(barrier, inc=1, device_id=(section, peer_at(k)), device_id_type=MESH)
        return carry

    def greet_sections(k, carry):
        pl.semaphore_signal(barrier, inc=1, device_id=(before, k), device_id_type=MESH)
        pl.semaphore_signal(barrier, inc=1, device_id=(after, k), device_id_type=MESH)
        return carry

    lax.fori_loop(0, n - 1, greet_peer, 0)
    lax.fori_loop(0, n, greet_sections, 0)
    pl.semaphore_wait(barrier, 3 * n - 1)

    def columns(owner, c):
        return pl.ds(pl.multiple_of((owner * heads + c * per_chunk) * DH, DH), per_chunk * DH)

    def span_rows(owner):
        return pl.ds(pl.multiple_of(past + owner * tok, 16), tok)

    def inputs(c, owner, rows):
        cols = columns(owner, c)
        return (
            (span_ref.at[:, :, cols], held.at[c, pl.ds(0, 3), span_rows(rows), :]),
            (dout_ref.at[:, cols], held.at[c, DOUT, span_rows(rows), :]),
        )

    def send_tokens(c, peer):
        return [
            pltpu.make_async_remote_copy(
                src_ref=source,
                dst_ref=target,
                send_sem=send_in.at[c, which, peer],
                recv_sem=recv_in.at[c, which, me],
                device_id=(section, peer),
                device_id_type=MESH,
            )
            for which, (source, target) in enumerate(inputs(c, peer, me))
        ]

    def receive_tokens(c, peer):
        return [
            pltpu.make_async_remote_copy(
                src_ref=source,
                dst_ref=target,
                send_sem=send_in.at[c, which, me],
                recv_sem=recv_in.at[c, which, peer],
                device_id=(section, peer),
                device_id_type=MESH,
            )
            for which, (source, target) in enumerate(inputs(c, me, peer))
        ]

    def own_tokens(c):
        return [
            pltpu.make_async_copy(source, target, own_sem.at[c, which])
            for which, (source, target) in enumerate(inputs(c, me, me))
        ]

    def slim(c, peer, rows, sender):
        cols = columns(peer, c)
        target = held.at[c, QUERY, span_rows(rows), :]
        dout_target = held.at[c, DOUT, span_rows(rows), :]
        return [
            pltpu.make_async_remote_copy(
                src_ref=source,
                dst_ref=destination,
                send_sem=send_in.at[c, which, peer],
                recv_sem=recv_in.at[c, which, rows],
                device_id=(section, sender),
                device_id_type=MESH,
            )
            for which, (source, destination) in enumerate(
                ((span_ref.at[QUERY, :, cols], target), (dout_ref.at[:, cols], dout_target))
            )
        ]

    def each_token_copy(c, peer, outward, act):
        full = send_tokens if outward else receive_tokens
        if not pair:
            for copy in full(c, peer):
                act(copy)
            return
        if outward:
            cut = in_pair & (peer < last)
        else:
            cut = (peer >= last) & (me < last)

        @pl.when(cut)
        def _():
            for copy in slim(c, peer, me, peer) if outward else slim(c, me, peer, peer):
                act(copy)

        @pl.when(jnp.logical_not(cut))
        def _():
            for copy in full(c, peer):
                act(copy)

    def head_columns(owner, c):
        return pl.ds(pl.multiple_of((owner * heads + c * per_chunk + core) * DH, DH), DH)

    def far_inputs(owner):
        rows = pl.ds(pl.multiple_of(tail + (owner - last) * tok, 16), tok)
        cols = pl.ds(0, last * heads * DH)
        return (
            (span_ref.at[:, :, cols], far.at[pl.ds(0, 3), rows, :]),
            (dout_ref.at[:, cols], far.at[DOUT, rows, :]),
        )

    def mate_copies(rows):
        return [
            pltpu.make_async_remote_copy(
                src_ref=source,
                dst_ref=target,
                send_sem=mate_send.at[which],
                recv_sem=mate_recv.at[which],
                device_id=(section, mate),
                device_id_type=MESH,
            )
            for which, (source, target) in enumerate(far_inputs(rows))
        ]

    def own_far():
        return [
            pltpu.make_async_copy(source, target, far_own.at[which])
            for which, (source, target) in enumerate(far_inputs(me))
        ]

    def send_stats(c, owner):
        return pltpu.make_async_remote_copy(
            src_ref=far_stats.at[c, owner],
            dst_ref=stats.at[c, core],
            send_sem=stats_send.at[c, owner],
            recv_sem=stats_recv.at[c, core],
            device_id=(section, owner),
            device_id_type=MESH,
        )

    def receive_stats(c, i):
        return pltpu.make_async_remote_copy(
            src_ref=far_stats.at[c, 0],
            dst_ref=stats.at[c, i],
            send_sem=stats_send.at[c, 0],
            recv_sem=stats_recv.at[c, i],
            device_id=(section, last + i),
            device_id_type=MESH,
        )

    def send_final(c, i, sender, target):
        lanes = pl.ds(i * DH, DH)
        return (
            pltpu.make_async_remote_copy(
                src_ref=final.at[c, i],
                dst_ref=far_final.at[c, sender],
                send_sem=final_send.at[c, i],
                recv_sem=final_recv.at[c, sender],
                device_id=(section, target),
                device_id_type=MESH,
            ),
            pltpu.make_async_remote_copy(
                src_ref=staged.at[c, 0, pl.ds(span - 2 * tok, 2 * tok), lanes],
                dst_ref=far_query.at[c, sender],
                send_sem=query_send.at[c, i],
                recv_sem=query_recv.at[c, sender],
                device_id=(section, target),
                device_id_type=MESH,
            ),
        )

    def send_far(c, owner, i):
        return pltpu.make_async_remote_copy(
            src_ref=far_out.at[c, owner, :, pl.ds(i * tok, tok), :],
            dst_ref=grads_ref.at[:, :, head_columns(owner, c)],
            send_sem=far_send.at[c, owner, i],
            recv_sem=recv_out.at[c, owner],
            device_id=(before, last + i),
            device_id_type=MESH,
        )

    def far_block(c, owner, length):
        lanes = head_columns(owner, c)
        keys, query = far[KEY, :, lanes], far[QUERY, :, lanes]
        masked, dprobs, dout = score_block(
            scale, tail, span - LANES, keys, far[VALUE, :, lanes], query, far[DOUT, :, lanes], length
        )
        return keys, query, masked, dprobs, dout

    def far_scores(length):
        def one(c, carry):
            found = []
            for owner in range(last):
                _, _, masked, dprobs, _ = far_block(c, owner, length)
                top = jnp.max(masked, axis=0, keepdims=True)
                exp_terms = jnp.exp(masked - top)
                total = jnp.sum(exp_terms, axis=0, keepdims=True)
                found.append((top, total, jnp.sum(exp_terms * dprobs, axis=0, keepdims=True)))
            for owner in range(last):
                for row in range(3):
                    far_stats[c, owner, row : row + 1, :] = found[owner][row]
                far_stats[c, owner, 3:8, :] = jnp.zeros((5, LANES), jnp.float32)
            for owner in range(last):
                send_stats(c, owner).start()
            return carry

        lax.fori_loop(0, chunks, one, 0)

    def far_grads(c, length):
        for owner in range(last):
            for copy in send_final(c, 0, owner, owner):
                copy.wait_recv()
        found = []
        for owner in range(last):
            keys, query, masked, dprobs, dout = far_block(c, owner, length)
            top = far_final[c, owner, 0:1, :]
            inverse = far_final[c, owner, 1:2, :]
            delta = far_final[c, owner, 2:3, :]
            attention = jnp.exp(masked - top) * inverse
            dscores = (attention * (dprobs - delta)).astype(jnp.bfloat16)
            grad_query = lax.dot_general(
                dscores, keys, OVER_FIRST, preferred_element_type=jnp.float32
            )
            grad_query = grad_query[tail:] * scale + far_query[c, owner].astype(jnp.float32)
            grad_keys = jnp.dot(dscores, query, preferred_element_type=jnp.float32) * scale
            grad_values = jnp.dot(
                attention.astype(jnp.bfloat16), dout, preferred_element_type=jnp.float32
            )
            found.append((grad_query, grad_keys[tail:], grad_values[tail:]))
        for owner in range(last):
            for kind in range(3):
                far_out[c, owner, kind] = found[owner][kind].astype(jnp.bfloat16)
        for owner in range(last):
            for i in range(2):
                send_far(c, owner, i).start()

    def send_grads(c, token_owner):
        rows = pl.ds(pl.multiple_of(token_owner * tok, 16), tok)
        return pltpu.make_async_remote_copy(
            src_ref=staged.at[c, :, rows, :],
            dst_ref=grads_ref.at[:, :, columns(me, c)],
            send_sem=send_out.at[c, token_owner],
            recv_sem=recv_out.at[c, me],
            device_id=(before, token_owner),
            device_id_type=MESH,
        )

    def send_relay(c, i, token_owner):
        rows = pl.ds(pl.multiple_of(token_owner * tok, 16), tok)
        return pltpu.make_async_remote_copy(
            src_ref=staged.at[c, :, rows, :],
            dst_ref=relay.at[c, i],
            send_sem=send_out.at[c, token_owner],
            recv_sem=relay_recv.at[c, i],
            device_id=(section, token_owner),
            device_id_type=MESH,
        )

    def send_on(c, i):
        return pltpu.make_async_remote_copy(
            src_ref=relay.at[c, i],
            dst_ref=grads_ref.at[:, :, columns(last + i, c)],
            send_sem=relay_send.at[c, i],
            recv_sem=recv_out.at[c, last + i],
            device_id=(before, me),
            device_id_type=MESH,
        )

    def hand_on(c):
        for i in range(2):
            pltpu.make_async_remote_copy(
                src_ref=staged.at[c, :, pl.ds(0, tok), :],
                dst_ref=relay.at[c, i],
                send_sem=send_out.at[c, 0],
                recv_sem=relay_recv.at[c, i],
                device_id=(section, last + i),
                device_id_type=MESH,
            ).wait_recv()
            send_on(c, i).start()

    def out_copy(c, token_owner, act):
        if not pair:
            act(send_grads(c, token_owner))
            return

        @pl.when(in_pair == (token_owner >= last))
        def _():
            act(send_grads(c, token_owner))

        @pl.when(in_pair & (token_owner < last))
        def _():
            act(send_relay(c, core, token_owner))

    def receive_grads(c, head_owner):
        return pltpu.make_async_remote_copy(
            src_ref=staged.at[c, :, pl.ds(0, tok), :],
            dst_ref=grads_ref.at[:, :, columns(head_owner, c)],
            send_sem=send_out.at[c, head_owner],
            recv_sem=recv_out.at[c, head_owner],
            device_id=(after, head_owner),
            device_id_type=MESH,
        )

    def start_chunk(c, carry):
        def start_peer(k, carry):
            each_token_copy(c, peer_at(k), True, lambda copy: copy.start())
            return carry

        lax.fori_loop(0, n - 1, start_peer, 0)
        for copy in own_tokens(c):
            copy.start()
        return carry

    load_offset.wait()
    load_length.wait()
    offset = small[0, 0]
    length = small[1, 0]
    lead = min(2, chunks)
    if pair:

        @pl.when(in_pair)
        def _():
            for copy in mate_copies(me) + own_far():
                copy.start()

    lax.fori_loop(0, lead, start_chunk, 0)
    if pair:
        edge = pl.ds(past + span - 2 * tok, 2 * tok)

        @pl.when(in_pair)
        def _():
            if tail:
                far[:, pl.ds(0, tail), :] = jnp.zeros((4, tail, far.shape[2]), jnp.bfloat16)
            row = lax.broadcasted_iota(jnp.int32, stats.shape, 2)
            stats[...] = jnp.where(row == 0, HIDDEN, 0.0)
            for copy in own_far():
                copy.wait()
            for copy in mate_copies(mate):
                copy.wait_recv()
            far_scores(length)

        @pl.when(jnp.logical_not(in_pair))
        def _():
            held[:, pl.ds(KEY, 2), edge, :] = jnp.zeros(
                (chunks, 2, 2 * tok, per_chunk * DH), jnp.bfloat16
            )


    load_cache.wait()
    cache_wide[...] = cache_low[...].astype(jnp.float32)
    for h in range(heads):
        for which in (KEY, VALUE):
            rows = pl.ds((which - KEY) * heads + h, past, stride=2 * heads)
            lanes = pl.ds(h % per_chunk * DH, DH)
            held[h // per_chunk, which, pl.ds(0, past), lanes] = cache_wide[rows, :].astype(jnp.bfloat16)
    load_accum.wait()

    blocks = span // block
    span_cut = length
    if pair:
        span_cut = jnp.where(in_pair, length, jnp.minimum(length, span - 2 * tok))

    def one_head(c, i):
        h = c * per_chunk + i
        lanes = pl.ds(i * DH, DH)
        keys = held[c, KEY, :, lanes]
        values = held[c, VALUE, :, lanes]

        def one_block(start):
            others = None
            if pair:
                ahead = jnp.zeros((1, span - LANES), jnp.float32)
                others = [
                    jnp.concatenate([ahead + fill, stats[c, i, row : row + 1, :]], axis=1)
                    for row, fill in enumerate((HIDDEN, 0.0, 0.0))
                ]
            grad_query, grad_keys, grad_values, ends = attention_grads(
                scale,
                past,
                keys,
                values,
                held[c, QUERY, pl.ds(past + start, block), lanes],
                held[c, DOUT, pl.ds(past + start, block), lanes],
                offset,
                length,
                start,
                span_cut,
                others,
            )
            if pair:
                for row, value in enumerate(ends):
                    final[c, i, row : row + 1, :] = value[:, span - LANES :]
                final[c, i, 3:8, :] = jnp.zeros((5, LANES), jnp.float32)
            staged[c, 0, pl.ds(start, block), lanes] = grad_query.astype(jnp.bfloat16)
            return grad_keys, grad_values

        if blocks == 1:
            grad_keys, grad_values = one_block(0)
        else:
            total_keys[...] = jnp.zeros_like(total_keys)
            total_values[...] = jnp.zeros_like(total_values)

            def step(b, carry):
                more_keys, more_values = one_block(pl.multiple_of(b * block, block))
                total_keys[...] += more_keys
                total_values[...] += more_values
                return carry

            lax.fori_loop(0, blocks, step, 0)
            grad_keys, grad_values = total_keys[...], total_values[...]
        staged[c, 1, :, lanes] = grad_keys[past:].astype(jnp.bfloat16)
        staged[c, 2, :, lanes] = grad_values[past:].astype(jnp.bfloat16)
        accum[pl.ds(h, past, stride=2 * heads), :] += grad_keys[:past]
        accum[pl.ds(heads + h, past, stride=2 * heads), :] += grad_values[:past]

    def work_chunk(c, carry):
        def wait_peer(k, carry):
            each_token_copy(c, peer_at(k), False, lambda copy: copy.wait_recv())
            return carry

        lax.fori_loop(0, n - 1, wait_peer, 0)
        for copy in own_tokens(c):
            copy.wait()

        if pair:

            @pl.when(jnp.logical_not(in_pair))
            def _():
                for i in range(2):
                    receive_stats(c, i).wait_recv()

        for i in range(per_chunk):
            one_head(c, i)

        if pair:

            @pl.when(jnp.logical_not(in_pair))
            def _():
                for i in range(2):
                    for copy in send_final(c, i, me, last + i):
                        copy.start()

        def start_out(k, carry):
            out_copy(c, peer_at(k), lambda copy: copy.start())
            return carry

        lax.fori_loop(0, n - 1, start_out, 0)
        send_grads(c, me).start()

        @pl.when(c + lead < chunks)
        def _():
            start_chunk(c + lead, 0)

        if pair:

            @pl.when(in_pair & (c > 0))
            def _():
                far_grads(c - 1, length)

            @pl.when(jnp.logical_not(in_pair) & (c > 0))
            def _():
                hand_on(c - 1)

        return carry

    lax.fori_loop(0, chunks, work_chunk, 0)

    store_accum = pltpu.make_async_copy(accum, new_accum_ref, io_sem.at[1])
    store_accum.start()
    if pair:

        @pl.when(in_pair)
        def _():
            far_grads(chunks - 1, length)
            for copy in mate_copies(me):
                copy.wait_send()

        @pl.when(jnp.logical_not(in_pair))
        def _():
            hand_on(chunks - 1)

    def finish_chunk(c, carry):
        def sent(k, carry):
            each_token_copy(c, peer_at(k), True, lambda copy: copy.wait_send())
            return carry

        def exchanged(t, carry):
            out_copy(c, t, lambda copy: copy.wait_send())
            receive_grads(c, t).wait_recv()
            return carry

        lax.fori_loop(0, n - 1, sent, 0)
        lax.fori_loop(0, n, exchanged, 0)
        if pair:

            @pl.when(jnp.logical_not(in_pair))
            def _():
                for i in range(2):
                    for copy in send_final(c, i, me, last + i):
                        copy.wait_send()
                    send_on(c, i).wait_send()

            @pl.when(in_pair)
            def _():
                def far_sent(owner, carry):
                    send_stats(c, owner).wait_send()
                    for i in range(2):
                        send_far(c, owner, i).wait_send()
                    return carry

                lax.fori_loop(0, last, far_sent, 0)

        return carry

    lax.fori_loop(0, chunks, finish_chunk, 0)
    store_accum.wait()


def per_device(sections, n, span_inputs, out_grad, past_cache, past_accum, offsets, lengths):
    _, tok, _, width = span_inputs.shape
    _, past, _, heads, dh = past_cache.shape
    span = tok * n
    key_count = past + span
    chunks = 4 if heads % 4 == 0 else 1
    block = min(span, 256 if key_count <= 1024 else 128)
    by_kind = span_inputs[0].transpose(1, 0, 2)
    cache_rows = past_cache.reshape(past * 2 * heads, dh)
    accum_rows = past_accum.reshape(past * 2 * heads, dh)
    dims = (sections, n, heads, tok, past, span, chunks, block)
    spread = (key_count, dh) if span > block else (8, dh)
    anywhere = pl.BlockSpec(memory_space=pl.ANY)
    resident = pl.BlockSpec(memory_space=pltpu.HBM)
    pair_scratch = []
    if heads // chunks == 2 and 2 * tok <= LANES <= span == block and n > 2 and n % 2 == 0:
        last = n - 2
        dma = pltpu.SemaphoreType.DMA
        pair_scratch = [
            pltpu.VMEM((4, LANES, last * heads * dh), jnp.bfloat16),
            pltpu.VMEM((chunks, last, 8, LANES), jnp.float32),
            pltpu.VMEM((chunks, last, 8, LANES), jnp.float32),
            pltpu.VMEM((chunks, last, 2 * tok, dh), jnp.bfloat16),
            pltpu.VMEM((chunks, last, 3, 2 * tok, dh), jnp.bfloat16),
            pltpu.VMEM((chunks, 2, 8, LANES), jnp.float32),
            pltpu.VMEM((chunks, 2, 8, LANES), jnp.float32),
            dma((2,)),
            dma((2,)),
            dma((2,)),
            dma((chunks, last)),
            dma((chunks, 2)),
            dma((chunks, 2)),
            dma((chunks, last)),
            dma((chunks, 2)),
            dma((chunks, last)),
            dma((chunks, last, 2)),
            pltpu.VMEM((chunks, 2, 3, tok, 2 * dh), jnp.bfloat16),
            dma((chunks, 2)),
            dma((chunks, 2)),
        ]
    pairs = heads * span * key_count * dh
    grads, new_rows = pl.pallas_call(
        functools.partial(kernel, dims),
        out_shape=(
            jax.ShapeDtypeStruct((3, tok, width), jnp.bfloat16),
            jax.ShapeDtypeStruct(accum_rows.shape, jnp.float32),
        ),
        in_specs=[resident, resident] + [anywhere] * 4,
        out_specs=(anywhere, anywhere),
        scratch_shapes=[
            pltpu.VMEM((chunks, 4, key_count, heads // chunks * dh), jnp.bfloat16),
            pltpu.VMEM((chunks, 3, span, heads // chunks * dh), jnp.bfloat16),
            pltpu.VMEM(cache_rows.shape, jnp.bfloat16),
            pltpu.VMEM(cache_rows.shape, jnp.float32),
            pltpu.VMEM(accum_rows.shape, jnp.float32),
            pltpu.VMEM(spread, jnp.float32),
            pltpu.VMEM(spread, jnp.float32),
            pltpu.SemaphoreType.DMA((chunks, 2, n)),
            pltpu.SemaphoreType.DMA((chunks, 2, n)),
            pltpu.SemaphoreType.DMA((chunks, n)),
            pltpu.SemaphoreType.DMA((chunks, n)),
            pltpu.SemaphoreType.DMA((chunks, 2)),
            pltpu.SemaphoreType.DMA((4,)),
            pltpu.SMEM((2, 1), jnp.int32),
            *pair_scratch,
        ],
        compiler_params=pltpu.CompilerParams(
            collective_id=0, has_side_effects=True, vmem_limit_bytes=56 * 1024 * 1024
        ),
        cost_estimate=pl.CostEstimate(
            flops=10 * pairs, bytes_accessed=16 * accum_rows.size, transcendentals=pairs // dh
        ),
    )(offsets, lengths, by_kind, out_grad[0], cache_rows, accum_rows)
    next_grads = grads.transpose(1, 0, 2)[None]
    return next_grads, new_rows.reshape(past_accum.shape)


def solution(mesh):
    in_specs = (
        P("section", "seq", None, None),
        P("section", "seq", None),
        P("section", None, None, "seq", None),
        P("section", None, None, "seq", None),
        P("section"),
        P("section"),
    )
    out_specs = (P("section", "seq", None, None), P("section", None, None, "seq", None))
    return jax.shard_map(
        functools.partial(per_device, mesh.shape["section"], mesh.shape["seq"]),
        mesh=mesh,
        in_specs=in_specs,
        out_specs=out_specs,
        check_vma=False,
    )
```

```python
import functools
import math

import jax
import jax.numpy as jnp
from jax import lax
from jax.experimental import pallas as pl
from jax.experimental.pallas import tpu as pltpu
from jax.sharding import PartitionSpec as P

DH = 128
MESH = pl.DeviceIdType.MESH
QUERY, KEY, VALUE, DOUT = range(4)


def attention_grads(scale, past, keys, values, query, dout, offset, length, start):
    key_count, rows = keys.shape[0], query.shape[0]
    key_index = lax.broadcasted_iota(jnp.int32, (key_count, rows), 0)
    query_pos = start + lax.broadcasted_iota(jnp.int32, (key_count, rows), 1)
    in_span = key_index - past
    limit = jnp.where(in_span < 0, offset - past, jnp.minimum(query_pos + 1, length))
    over_last = (((1,), (1,)), ((), ()))
    scores = lax.dot_general(keys, query, over_last, preferred_element_type=jnp.float32) * scale
    masked = jnp.where(in_span < limit, scores, -jnp.inf)
    exp_terms = jnp.exp(masked - jnp.max(masked, axis=0, keepdims=True))
    attention = exp_terms * (1.0 / jnp.sum(exp_terms, axis=0, keepdims=True))
    row_pos = start + lax.broadcasted_iota(jnp.int32, (rows, DH), 0)
    dout = jnp.where(row_pos < length, dout, jnp.zeros_like(dout))
    dprobs = lax.dot_general(values, dout, over_last, preferred_element_type=jnp.float32)
    delta = jnp.sum(attention * dprobs, axis=0, keepdims=True)
    dscores = (attention * (dprobs - delta)).astype(jnp.bfloat16)
    grad_values = jnp.dot(
        attention.astype(jnp.bfloat16), dout, preferred_element_type=jnp.float32
    )
    grad_keys = jnp.dot(dscores, query, preferred_element_type=jnp.float32) * scale
    grad_query = (
        lax.dot_general(
            dscores, keys, (((0,), (0,)), ((), ())), preferred_element_type=jnp.float32
        )
        * scale
    )
    return grad_query, grad_keys, grad_values


def kernel(
    dims,
    offset_ref,
    length_ref,
    span_ref,
    dout_ref,
    cache_ref,
    accum_ref,
    grads_ref,
    new_accum_ref,
    held,
    staged,
    cache_low,
    cache_wide,
    accum,
    total_keys,
    total_values,
    send_in,
    recv_in,
    send_out,
    recv_out,
    own_sem,
    io_sem,
    small,
):
    sections, n, heads, tok, past, span, chunks, block = dims
    per_chunk = heads // chunks
    scale = 1.0 / math.sqrt(DH)
    me = lax.axis_index("seq")
    section = lax.axis_index("section")
    before = lax.rem(section + sections - 1, sections)
    after = lax.rem(section + 1, sections)

    load_cache = pltpu.make_async_copy(cache_ref, cache_low, io_sem.at[0])
    load_accum = pltpu.make_async_copy(accum_ref, accum, io_sem.at[1])
    load_offset = pltpu.make_async_copy(offset_ref, small.at[0], io_sem.at[2])
    load_length = pltpu.make_async_copy(length_ref, small.at[1], io_sem.at[3])
    load_cache.start()
    load_accum.start()
    load_offset.start()
    load_length.start()

    def peer_at(k):
        half = n // 2
        mine = me // half
        far = (1 - mine) * half + lax.rem(me + k, half)
        near = mine * half + lax.rem(me + k - half + 1, half)
        return jnp.where(k < half, far, near)

    barrier = pltpu.get_barrier_semaphore()

    def greet_peer(k, carry):
        pl.semaphore_signal(barrier, inc=1, device_id=(section, peer_at(k)), device_id_type=MESH)
        return carry

    def greet_sections(k, carry):
        pl.semaphore_signal(barrier, inc=1, device_id=(before, k), device_id_type=MESH)
        pl.semaphore_signal(barrier, inc=1, device_id=(after, k), device_id_type=MESH)
        return carry

    lax.fori_loop(0, n - 1, greet_peer, 0)
    lax.fori_loop(0, n, greet_sections, 0)
    pl.semaphore_wait(barrier, 3 * n - 1)

    def columns(owner, c):
        return pl.ds(pl.multiple_of((owner * heads + c * per_chunk) * DH, DH), per_chunk * DH)

    def span_rows(owner):
        return pl.ds(pl.multiple_of(past + owner * tok, 16), tok)

    def inputs(c, owner, rows):
        cols = columns(owner, c)
        return (
            (span_ref.at[:, :, cols], held.at[c, pl.ds(0, 3), span_rows(rows), :]),
            (dout_ref.at[:, cols], held.at[c, DOUT, span_rows(rows), :]),
        )

    def send_tokens(c, peer):
        return [
            pltpu.make_async_remote_copy(
                src_ref=source,
                dst_ref=target,
                send_sem=send_in.at[c, which, peer],
                recv_sem=recv_in.at[c, which, me],
                device_id=(section, peer),
                device_id_type=MESH,
            )
            for which, (source, target) in enumerate(inputs(c, peer, me))
        ]

    def receive_tokens(c, peer):
        return [
            pltpu.make_async_remote_copy(
                src_ref=source,
                dst_ref=target,
                send_sem=send_in.at[c, which, me],
                recv_sem=recv_in.at[c, which, peer],
                device_id=(section, peer),
                device_id_type=MESH,
            )
            for which, (source, target) in enumerate(inputs(c, me, peer))
        ]

    def own_tokens(c):
        return [
            pltpu.make_async_copy(source, target, own_sem.at[c, which])
            for which, (source, target) in enumerate(inputs(c, me, me))
        ]

    def send_grads(c, token_owner):
        rows = pl.ds(pl.multiple_of(token_owner * tok, 16), tok)
        return pltpu.make_async_remote_copy(
            src_ref=staged.at[c, :, rows, :],
            dst_ref=grads_ref.at[:, :, columns(me, c)],
            send_sem=send_out.at[c, token_owner],
            recv_sem=recv_out.at[c, me],
            device_id=(before, token_owner),
            device_id_type=MESH,
        )

    def receive_grads(c, head_owner):
        return pltpu.make_async_remote_copy(
            src_ref=staged.at[c, :, pl.ds(0, tok), :],
            dst_ref=grads_ref.at[:, :, columns(head_owner, c)],
            send_sem=send_out.at[c, head_owner],
            recv_sem=recv_out.at[c, head_owner],
            device_id=(after, head_owner),
            device_id_type=MESH,
        )

    def start_chunk(c, carry):
        def start_peer(k, carry):
            for copy in send_tokens(c, peer_at(k)):
                copy.start()
            return carry

        lax.fori_loop(0, n - 1, start_peer, 0)
        for copy in own_tokens(c):
            copy.start()
        return carry

    lead = min(3, chunks)
    lax.fori_loop(0, lead, start_chunk, 0)

    load_cache.wait()
    cache_wide[...] = cache_low[...].astype(jnp.float32)
    for h in range(heads):
        for which in (KEY, VALUE):
            rows = pl.ds((which - KEY) * heads + h, past, stride=2 * heads)
            lanes = pl.ds(h % per_chunk * DH, DH)
            held[h // per_chunk, which, pl.ds(0, past), lanes] = cache_wide[rows, :].astype(jnp.bfloat16)
    load_accum.wait()

    load_offset.wait()
    load_length.wait()
    offset = small[0, 0]
    length = small[1, 0]
    blocks = span // block

    def one_head(c, i):
        h = c * per_chunk + i
        lanes = pl.ds(pl.multiple_of(i * DH, DH), DH)
        keys = held[c, KEY, :, lanes]
        values = held[c, VALUE, :, lanes]

        def one_block(start):
            grad_query, grad_keys, grad_values = attention_grads(
                scale,
                past,
                keys,
                values,
                held[c, QUERY, pl.ds(past + start, block), lanes],
                held[c, DOUT, pl.ds(past + start, block), lanes],
                offset,
                length,
                start,
            )
            staged[c, 0, pl.ds(start, block), lanes] = grad_query.astype(jnp.bfloat16)
            return grad_keys, grad_values

        if blocks == 1:
            grad_keys, grad_values = one_block(0)
        else:
            total_keys[...] = jnp.zeros_like(total_keys)
            total_values[...] = jnp.zeros_like(total_values)

            def step(b, carry):
                more_keys, more_values = one_block(pl.multiple_of(b * block, block))
                total_keys[...] += more_keys
                total_values[...] += more_values
                return carry

            lax.fori_loop(0, blocks, step, 0)
            grad_keys, grad_values = total_keys[...], total_values[...]
        staged[c, 1, :, lanes] = grad_keys[past:].astype(jnp.bfloat16)
        staged[c, 2, :, lanes] = grad_values[past:].astype(jnp.bfloat16)
        accum[pl.ds(h, past, stride=2 * heads), :] += grad_keys[:past]
        accum[pl.ds(heads + h, past, stride=2 * heads), :] += grad_values[:past]

    def work_chunk(c, carry):
        def wait_peer(k, carry):
            for copy in receive_tokens(c, peer_at(k)):
                copy.wait_recv()
            return carry

        lax.fori_loop(0, n - 1, wait_peer, 0)
        for copy in own_tokens(c):
            copy.wait()

        def work_head(i, carry):
            one_head(c, i)
            return carry

        lax.fori_loop(0, per_chunk, work_head, 0)

        def start_out(k, carry):
            send_grads(c, peer_at(k)).start()
            return carry

        lax.fori_loop(0, n - 1, start_out, 0)
        send_grads(c, me).start()

        @pl.when(c + lead < chunks)
        def _():
            start_chunk(c + lead, 0)

        return carry

    lax.fori_loop(0, chunks, work_chunk, 0)

    store_accum = pltpu.make_async_copy(accum, new_accum_ref, io_sem.at[1])
    store_accum.start()

    def finish_chunk(c, carry):
        def sent(k, carry):
            for copy in send_tokens(c, peer_at(k)):
                copy.wait_send()
            return carry

        def exchanged(t, carry):
            send_grads(c, t).wait_send()
            receive_grads(c, t).wait_recv()
            return carry

        lax.fori_loop(0, n - 1, sent, 0)
        lax.fori_loop(0, n, exchanged, 0)
        return carry

    lax.fori_loop(0, chunks, finish_chunk, 0)
    store_accum.wait()


def per_device(sections, n, span_inputs, out_grad, past_cache, past_accum, offsets, lengths):
    _, tok, _, width = span_inputs.shape
    _, past, _, heads, dh = past_cache.shape
    span = tok * n
    key_count = past + span
    chunks = heads
    block = min(span, 256 if key_count <= 1024 else 128)
    by_kind = span_inputs[0].transpose(1, 0, 2)
    cache_rows = past_cache.reshape(past * 2 * heads, dh)
    accum_rows = past_accum.reshape(past * 2 * heads, dh)
    dims = (sections, n, heads, tok, past, span, chunks, block)
    spread = (key_count, dh) if span > block else (8, dh)
    anywhere = pl.BlockSpec(memory_space=pl.ANY)
    resident = pl.BlockSpec(memory_space=pltpu.HBM)
    pairs = heads * span * key_count * dh
    grads, new_rows = pl.pallas_call(
        functools.partial(kernel, dims),
        out_shape=(
            jax.ShapeDtypeStruct((3, tok, width), jnp.bfloat16),
            jax.ShapeDtypeStruct(accum_rows.shape, jnp.float32),
        ),
        in_specs=[resident, resident] + [anywhere] * 4,
        out_specs=(anywhere, anywhere),
        scratch_shapes=[
            pltpu.VMEM((chunks, 4, key_count, heads // chunks * dh), jnp.bfloat16),
            pltpu.VMEM((chunks, 3, span, heads // chunks * dh), jnp.bfloat16),
            pltpu.VMEM(cache_rows.shape, jnp.bfloat16),
            pltpu.VMEM(cache_rows.shape, jnp.float32),
            pltpu.VMEM(accum_rows.shape, jnp.float32),
            pltpu.VMEM(spread, jnp.float32),
            pltpu.VMEM(spread, jnp.float32),
            pltpu.SemaphoreType.DMA((chunks, 2, n)),
            pltpu.SemaphoreType.DMA((chunks, 2, n)),
            pltpu.SemaphoreType.DMA((chunks, n)),
            pltpu.SemaphoreType.DMA((chunks, n)),
            pltpu.SemaphoreType.DMA((chunks, 2)),
            pltpu.SemaphoreType.DMA((4,)),
            pltpu.SMEM((2, 1), jnp.int32),
        ],
        compiler_params=pltpu.CompilerParams(
            collective_id=0, has_side_effects=True, vmem_limit_bytes=56 * 1024 * 1024
        ),
        cost_estimate=pl.CostEstimate(
            flops=10 * pairs, bytes_accessed=16 * accum_rows.size, transcendentals=pairs // dh
        ),
    )(offsets, lengths, by_kind, out_grad[0], cache_rows, accum_rows)
    next_grads = grads.transpose(1, 0, 2)[None]
    return next_grads, new_rows.reshape(past_accum.shape)


def solution(mesh):
    in_specs = (
        P("section", "seq", None, None),
        P("section", "seq", None),
        P("section", None, None, "seq", None),
        P("section", None, None, "seq", None),
        P("section"),
        P("section"),
    )
    out_specs = (P("section", "seq", None, None), P("section", None, None, "seq", None))
    return jax.shard_map(
        functools.partial(per_device, mesh.shape["section"], mesh.shape["seq"]),
        mesh=mesh,
        in_specs=in_specs,
        out_specs=out_specs,
        check_vma=False,
    )
```

```python
import functools
import math

import jax
import jax.numpy as jnp
from jax import lax
from jax.experimental import pallas as pl
from jax.experimental.pallas import tpu as pltpu
from jax.sharding import PartitionSpec as P

DH = 128
MESH = pl.DeviceIdType.MESH
QUERY, KEY, VALUE, DOUT = range(4)


def attention_grads(scale, past, keys, values, query, dout, offset, length, start):
    key_count, rows = keys.shape[0], query.shape[0]
    key_index = lax.broadcasted_iota(jnp.int32, (key_count, rows), 0)
    query_pos = start + lax.broadcasted_iota(jnp.int32, (key_count, rows), 1)
    in_span = key_index - past
    limit = jnp.where(in_span < 0, offset - past, jnp.minimum(query_pos + 1, length))
    over_last = (((1,), (1,)), ((), ()))
    scores = lax.dot_general(keys, query, over_last, preferred_element_type=jnp.float32) * scale
    masked = jnp.where(in_span < limit, scores, -jnp.inf)
    exp_terms = jnp.exp(masked - jnp.max(masked, axis=0, keepdims=True))
    attention = exp_terms * (1.0 / jnp.sum(exp_terms, axis=0, keepdims=True))
    row_pos = start + lax.broadcasted_iota(jnp.int32, (rows, DH), 0)
    dout = jnp.where(row_pos < length, dout, jnp.zeros_like(dout))
    dprobs = lax.dot_general(values, dout, over_last, preferred_element_type=jnp.float32)
    delta = jnp.sum(attention * dprobs, axis=0, keepdims=True)
    dscores = (attention * (dprobs - delta)).astype(jnp.bfloat16)
    grad_values = jnp.dot(
        attention.astype(jnp.bfloat16), dout, preferred_element_type=jnp.float32
    )
    grad_keys = jnp.dot(dscores, query, preferred_element_type=jnp.float32) * scale
    grad_query = (
        lax.dot_general(
            dscores, keys, (((0,), (0,)), ((), ())), preferred_element_type=jnp.float32
        )
        * scale
    )
    return grad_query, grad_keys, grad_values


def kernel(
    dims,
    offset_ref,
    length_ref,
    span_ref,
    dout_ref,
    cache_ref,
    accum_ref,
    grads_ref,
    new_accum_ref,
    held,
    staged,
    cache_low,
    cache_wide,
    accum,
    total_keys,
    total_values,
    send_in,
    recv_in,
    send_out,
    recv_out,
    own_sem,
    io_sem,
    small,
):
    sections, n, heads, tok, past, span, chunks, block = dims
    per_chunk = heads // chunks
    scale = 1.0 / math.sqrt(DH)
    me = lax.axis_index("seq")
    section = lax.axis_index("section")
    before = lax.rem(section + sections - 1, sections)
    after = lax.rem(section + 1, sections)

    load_cache = pltpu.make_async_copy(cache_ref, cache_low, io_sem.at[0])
    load_accum = pltpu.make_async_copy(accum_ref, accum, io_sem.at[1])
    load_offset = pltpu.make_async_copy(offset_ref, small.at[0], io_sem.at[2])
    load_length = pltpu.make_async_copy(length_ref, small.at[1], io_sem.at[3])
    load_cache.start()
    load_accum.start()
    load_offset.start()
    load_length.start()

    def peer_at(k):
        half = n // 2
        mine = me // half
        far = (1 - mine) * half + lax.rem(me + k, half)
        near = mine * half + lax.rem(me + k - half + 1, half)
        return jnp.where(k < half, far, near)

    barrier = pltpu.get_barrier_semaphore()

    def greet_peer(k, carry):
        pl.semaphore_signal(barrier, inc=1, device_id=(section, peer_at(k)), device_id_type=MESH)
        return carry

    def greet_sections(k, carry):
        pl.semaphore_signal(barrier, inc=1, device_id=(before, k), device_id_type=MESH)
        pl.semaphore_signal(barrier, inc=1, device_id=(after, k), device_id_type=MESH)
        return carry

    lax.fori_loop(0, n - 1, greet_peer, 0)
    lax.fori_loop(0, n, greet_sections, 0)
    pl.semaphore_wait(barrier, 3 * n - 1)

    def columns(owner, c):
        return pl.ds(pl.multiple_of((owner * heads + c * per_chunk) * DH, DH), per_chunk * DH)

    def span_rows(owner):
        return pl.ds(pl.multiple_of(past + owner * tok, 16), tok)

    def inputs(c, owner, rows):
        cols = columns(owner, c)
        return (
            (span_ref.at[:, :, cols], held.at[c, pl.ds(0, 3), span_rows(rows), :]),
            (dout_ref.at[:, cols], held.at[c, DOUT, span_rows(rows), :]),
        )

    def send_tokens(c, peer):
        return [
            pltpu.make_async_remote_copy(
                src_ref=source,
                dst_ref=target,
                send_sem=send_in.at[c, which, peer],
                recv_sem=recv_in.at[c, which, me],
                device_id=(section, peer),
                device_id_type=MESH,
            )
            for which, (source, target) in enumerate(inputs(c, peer, me))
        ]

    def receive_tokens(c, peer):
        return [
            pltpu.make_async_remote_copy(
                src_ref=source,
                dst_ref=target,
                send_sem=send_in.at[c, which, me],
                recv_sem=recv_in.at[c, which, peer],
                device_id=(section, peer),
                device_id_type=MESH,
            )
            for which, (source, target) in enumerate(inputs(c, me, peer))
        ]

    def own_tokens(c):
        return [
            pltpu.make_async_copy(source, target, own_sem.at[c, which])
            for which, (source, target) in enumerate(inputs(c, me, me))
        ]

    def send_grads(c, token_owner):
        rows = pl.ds(pl.multiple_of(token_owner * tok, 16), tok)
        return pltpu.make_async_remote_copy(
            src_ref=staged.at[c, :, rows, :],
            dst_ref=grads_ref.at[:, :, columns(me, c)],
            send_sem=send_out.at[c, token_owner],
            recv_sem=recv_out.at[c, me],
            device_id=(before, token_owner),
            device_id_type=MESH,
        )

    def receive_grads(c, head_owner):
        return pltpu.make_async_remote_copy(
            src_ref=staged.at[c, :, pl.ds(0, tok), :],
            dst_ref=grads_ref.at[:, :, columns(head_owner, c)],
            send_sem=send_out.at[c, head_owner],
            recv_sem=recv_out.at[c, head_owner],
            device_id=(after, head_owner),
            device_id_type=MESH,
        )

    def start_chunk(c, carry):
        def start_peer(k, carry):
            for copy in send_tokens(c, peer_at(k)):
                copy.start()
            return carry

        lax.fori_loop(0, n - 1, start_peer, 0)
        for copy in own_tokens(c):
            copy.start()
        return carry

    lead = min(2, chunks)
    lax.fori_loop(0, lead, start_chunk, 0)

    load_cache.wait()
    cache_wide[...] = cache_low[...].astype(jnp.float32)
    for h in range(heads):
        for which in (KEY, VALUE):
            rows = pl.ds((which - KEY) * heads + h, past, stride=2 * heads)
            lanes = pl.ds(h % per_chunk * DH, DH)
            held[h // per_chunk, which, pl.ds(0, past), lanes] = cache_wide[rows, :].astype(jnp.bfloat16)
    load_accum.wait()

    load_offset.wait()
    load_length.wait()
    offset = small[0, 0]
    length = small[1, 0]
    blocks = span // block

    def one_head(c, i):
        h = c * per_chunk + i
        lanes = pl.ds(pl.multiple_of(i * DH, DH), DH)
        keys = held[c, KEY, :, lanes]
        values = held[c, VALUE, :, lanes]

        def one_block(start):
            grad_query, grad_keys, grad_values = attention_grads(
                scale,
                past,
                keys,
                values,
                held[c, QUERY, pl.ds(past + start, block), lanes],
                held[c, DOUT, pl.ds(past + start, block), lanes],
                offset,
                length,
                start,
            )
            staged[c, 0, pl.ds(start, block), lanes] = grad_query.astype(jnp.bfloat16)
            return grad_keys, grad_values

        if blocks == 1:
            grad_keys, grad_values = one_block(0)
        else:
            total_keys[...] = jnp.zeros_like(total_keys)
            total_values[...] = jnp.zeros_like(total_values)

            def step(b, carry):
                more_keys, more_values = one_block(pl.multiple_of(b * block, block))
                total_keys[...] += more_keys
                total_values[...] += more_values
                return carry

            lax.fori_loop(0, blocks, step, 0)
            grad_keys, grad_values = total_keys[...], total_values[...]
        staged[c, 1, :, lanes] = grad_keys[past:].astype(jnp.bfloat16)
        staged[c, 2, :, lanes] = grad_values[past:].astype(jnp.bfloat16)
        accum[pl.ds(h, past, stride=2 * heads), :] += grad_keys[:past]
        accum[pl.ds(heads + h, past, stride=2 * heads), :] += grad_values[:past]

    def work_chunk(c, carry):
        def wait_peer(k, carry):
            for copy in receive_tokens(c, peer_at(k)):
                copy.wait_recv()
            return carry

        lax.fori_loop(0, n - 1, wait_peer, 0)
        for copy in own_tokens(c):
            copy.wait()

        def work_head(i, carry):
            one_head(c, i)
            return carry

        lax.fori_loop(0, per_chunk, work_head, 0)

        def start_out(k, carry):
            send_grads(c, peer_at(k)).start()
            return carry

        lax.fori_loop(0, n - 1, start_out, 0)
        send_grads(c, me).start()

        @pl.when(c + lead < chunks)
        def _():
            start_chunk(c + lead, 0)

        return carry

    lax.fori_loop(0, chunks, work_chunk, 0)

    store_accum = pltpu.make_async_copy(accum, new_accum_ref, io_sem.at[1])
    store_accum.start()

    def finish_chunk(c, carry):
        def sent(k, carry):
            for copy in send_tokens(c, peer_at(k)):
                copy.wait_send()
            return carry

        def exchanged(t, carry):
            send_grads(c, t).wait_send()
            receive_grads(c, t).wait_recv()
            return carry

        lax.fori_loop(0, n - 1, sent, 0)
        lax.fori_loop(0, n, exchanged, 0)
        return carry

    lax.fori_loop(0, chunks, finish_chunk, 0)
    store_accum.wait()


def per_device(sections, n, span_inputs, out_grad, past_cache, past_accum, offsets, lengths):
    _, tok, _, width = span_inputs.shape
    _, past, _, heads, dh = past_cache.shape
    span = tok * n
    key_count = past + span
    chunks = 4 if heads % 4 == 0 else 1
    block = min(span, 256 if key_count <= 1024 else 128)
    by_kind = span_inputs[0].transpose(1, 0, 2)
    cache_rows = past_cache.reshape(past * 2 * heads, dh)
    accum_rows = past_accum.reshape(past * 2 * heads, dh)
    dims = (sections, n, heads, tok, past, span, chunks, block)
    spread = (key_count, dh) if span > block else (8, dh)
    anywhere = pl.BlockSpec(memory_space=pl.ANY)
    resident = pl.BlockSpec(memory_space=pltpu.HBM)
    pairs = heads * span * key_count * dh
    grads, new_rows = pl.pallas_call(
        functools.partial(kernel, dims),
        out_shape=(
            pltpu.VMEM((3, tok, width), jnp.bfloat16),
            pltpu.VMEM(accum_rows.shape, jnp.float32),
        ),
        in_specs=[resident, resident] + [anywhere] * 4,
        out_specs=(anywhere, anywhere),
        scratch_shapes=[
            pltpu.VMEM((chunks, 4, key_count, heads // chunks * dh), jnp.bfloat16),
            pltpu.VMEM((chunks, 3, span, heads // chunks * dh), jnp.bfloat16),
            pltpu.VMEM(cache_rows.shape, jnp.bfloat16),
            pltpu.VMEM(cache_rows.shape, jnp.float32),
            pltpu.VMEM(accum_rows.shape, jnp.float32),
            pltpu.VMEM(spread, jnp.float32),
            pltpu.VMEM(spread, jnp.float32),
            pltpu.SemaphoreType.DMA((chunks, 2, n)),
            pltpu.SemaphoreType.DMA((chunks, 2, n)),
            pltpu.SemaphoreType.DMA((chunks, n)),
            pltpu.SemaphoreType.DMA((chunks, n)),
            pltpu.SemaphoreType.DMA((chunks, 2)),
            pltpu.SemaphoreType.DMA((4,)),
            pltpu.SMEM((2, 1), jnp.int32),
        ],
        compiler_params=pltpu.CompilerParams(
            collective_id=0, has_side_effects=True, vmem_limit_bytes=58 * 1024 * 1024
        ),
        cost_estimate=pl.CostEstimate(
            flops=10 * pairs, bytes_accessed=16 * accum_rows.size, transcendentals=pairs // dh
        ),
    )(offsets, lengths, by_kind, out_grad[0], cache_rows, accum_rows)
    next_grads = grads.transpose(1, 0, 2)[None]
    return next_grads, new_rows.reshape(past_accum.shape)


def solution(mesh):
    in_specs = (
        P("section", "seq", None, None),
        P("section", "seq", None),
        P("section", None, None, "seq", None),
        P("section", None, None, "seq", None),
        P("section"),
        P("section"),
    )
    out_specs = (P("section", "seq", None, None), P("section", None, None, "seq", None))
    return jax.shard_map(
        functools.partial(per_device, mesh.shape["section"], mesh.shape["seq"]),
        mesh=mesh,
        in_specs=in_specs,
        out_specs=out_specs,
        check_vma=False,
    )
```
